256 devices in a mesh: acq: 8 (over y, z_lo), tile: 32 (over x, z_hi, core).
Axes of the slice: x: 4, y: 4, z: 8 (z_hi: 4, z_lo: 2; z = z_hi * 2 + z_lo), core: 2. Of those that a mesh axis runs over, the one named last changes fastest.
Arguments:
- unprocessed_echo_data: float32 [2, 8, 768, 12288], P(None, 'acq', 'tile'), may hold values from -6 to 6
- slant_kernel_frequencies: float32 [2, 8, 12288], P(None, 'acq'), may hold values from -6 to 6
- along_track_kernel_angle: float32 [8, 768, 12288], P('acq', None, 'tile'), may hold values from -3.140625 to 3.140625
- pairs: int32 [2, 8], replicated, may hold values from 0 to 7, as said below
Outputs:
- interferogram: float32 [2, 2, 8, 128, 1536], P(None, None, 'acq', 'tile')
The draws below stay inside these ranges and needn't reach their ends.
Inputs may be any that keep to these rules, and one draw needn't show every extreme that they name: `pairs`: in each of the 2 rounds the partners of the 8 acquisitions are a permutation of them; an acquisition may be its own partner.
All inputs are finite; a program needn't handle non-finite values.
Results may differ from the reference program's by a relative error of at most 0.000098.
Values sent between devices are 32-bit elements; how exact they have to be, the bound alone decides.
A program may use at most 128 MiB of HBM per device.

```python
import jax
import jax.numpy as jnp
from jax import lax

NA = 768
NR = 12288
ROUNDS = 2
LOOK_AZ = 2
LOOK_RG = 8
AOI = 256
ACQ = 8
AOI_START = 256


def draw_pairs(key, part):
    round_rows = []
    for round_id in range(ROUNDS):
        partner_row = jax.random.permutation(jax.random.fold_in(key, 11 + round_id), ACQ).astype(jnp.int32)
        round_rows.append(partner_row)
    return jnp.stack(round_rows)


def steps_of(own_key, extent, shards, smallest, largest):
    gain, own = 1.0, jax.random.fold_in(own_key, 6)
    for dim, parts in shards:
        draws = jnp.exp(jax.random.uniform(jax.random.fold_in(own, dim), (parts,), jnp.float32, smallest / len(shards), largest / len(shards)))
        gain = gain * jnp.repeat(draws, extent[dim] // parts).reshape([-1 if axis == dim else 1 for axis in range(len(extent))])
    return gain


def gaussian(rng, shape, deviation, reach, shards=(), kind=jnp.bfloat16):
    level = steps_of(rng, shape, shards, -0.22, 0.18) if shards else 1.0
    drawn = jax.random.normal(rng, shape, jnp.float32) * deviation * level
    return jnp.minimum(jnp.maximum(drawn, -reach), reach).astype(kind)


def setup_inputs(seed: int = 0) -> dict:
    streams_of = jax.random.split(jax.random.key(seed), 5)
    return {
        "unprocessed_echo_data": gaussian(streams_of[0], (2, ACQ, NA, NR), 1.0, 6.0, ((1, 8), (2, 32)), jnp.float32),
        "slant_kernel_frequencies": gaussian(streams_of[1], (2, ACQ, NR), 0.7071, 6.0, ((1, 8),), jnp.float32),
        "along_track_kernel_angle": jnp.clip(jax.random.uniform(streams_of[2], (ACQ, NA, NR), jnp.float32, -3.140625, 3.140625), -3.140625, 3.140625),
        "pairs": draw_pairs(jax.random.fold_in(streams_of[4], 71), 0),
    }


def sharpen_one_scene(scene_collection):
    echo_inphase, echo_quadrature, kernel_inphase, kernel_quadrature, angle_term = scene_collection
    signal = lax.complex(echo_inphase, echo_quadrature)
    spectrum = jnp.fft.fft(signal, axis=1) * lax.complex(kernel_inphase, kernel_quadrature)[None, :]
    range_lines = jnp.fft.ifft(spectrum, axis=1)
    doppler = jnp.fft.fft(range_lines, axis=0) * lax.complex(jnp.cos(angle_term), jnp.sin(angle_term))
    sharpened_scene = jnp.fft.ifft(doppler, axis=0)[AOI_START:AOI_START + AOI]
    return jnp.stack([jnp.real(sharpened_scene), jnp.imag(sharpened_scene)])


def multilook(field):
    shaped = field.reshape(ROUNDS, ACQ, AOI // LOOK_AZ, LOOK_AZ, NR // LOOK_RG, LOOK_RG)
    return jnp.sum(shaped, axis=(3, 5)) / (LOOK_AZ * LOOK_RG)


def reference(unprocessed_echo_data, slant_kernel_frequencies, along_track_kernel_angle, pairs):
    sharpened_scene = lax.map(sharpen_one_scene, (unprocessed_echo_data[0], unprocessed_echo_data[1], slant_kernel_frequencies[0], slant_kernel_frequencies[1], along_track_kernel_angle))
    others = sharpened_scene[pairs]
    mine = sharpened_scene[None]
    cross_real = mine[:, :, 0] * others[:, :, 0] + mine[:, :, 1] * others[:, :, 1]
    cross_imag = mine[:, :, 1] * others[:, :, 0] - mine[:, :, 0] * others[:, :, 1]
    return jnp.stack([multilook(cross_real), multilook(cross_imag)])
```

```python
import jax
import jax.numpy as jnp
import ml_dtypes
import numpy as np
from jax import lax
from jax.experimental import pallas as pl
from jax.experimental.pallas import tpu as pltpu
from jax.sharding import PartitionSpec as P

MESH = pl.DeviceIdType.MESH
NA, NR, AOI, AOI_START = 768, 12288, 256, 256
NP, NQ = 96, 128
NB = 256
ACQ, TILE = 8, 32
GROUPS = 3
CHUNKS = 3
FIRST = AOI_START // 3
KEPT = 88
PART = AOI // ACQ
DESTS = TILE


def split3(matrix):
    high = matrix.astype(ml_dtypes.bfloat16)
    low = (matrix - high.astype(np.float64)).astype(ml_dtypes.bfloat16)
    return np.concatenate([high, high, low], axis=1).astype(np.float32)


def dft_block(size):
    ids = np.arange(size)
    angle = 2.0 * np.pi * (np.outer(ids, ids) % size) / size
    c, s = np.cos(angle), np.sin(angle)
    return np.block([[c, s], [-s, c]])


def tables():
    left_p = split3(dft_block(NP))
    right_q = dft_block(NQ).T.astype(np.float32)
    left_b = dft_block(NB).astype(np.float32)
    angle = 2.0 * np.pi * np.outer(np.arange(NP), np.arange(NQ)) / NR
    twist = np.stack([np.cos(angle), -np.sin(angle)]).astype(np.float32)
    column = np.zeros((NB, 128), np.float64)
    ids = np.arange(NB)
    for a in (1, 2):
        column[:, 2 * a - 2] = np.cos(2.0 * np.pi * a * ids / NA)
        column[:, 2 * a - 1] = -np.sin(2.0 * np.pi * a * ids / NA)
    pool = np.zeros((CHUNKS, 2, 128, 128), np.float32)
    for j in range(CHUNKS):
        for c in range(2):
            for n in range(128):
                pool[j, c, n, 64 * c + 16 * j + n // 8] = 1.0 / 16.0
    return left_p, right_q, left_b, twist, column.astype(np.float32), pool.reshape(CHUNKS, 256, 128)


def halves(value):
    high = value.astype(jnp.bfloat16)
    return high, (value - high.astype(jnp.float32)).astype(jnp.bfloat16)


def left_product(table, value):
    high, low = halves(value)
    rhs = jnp.concatenate([high, low, high], axis=0)
    return jnp.dot(table, rhs, preferred_element_type=jnp.float32)


def right_product(value, table):
    high, low = halves(value)
    lhs = jnp.concatenate([high, low, high], axis=1)
    return jnp.dot(lhs, table, preferred_element_type=jnp.float32)


def kernel(
    pairs, echo, filt, angle, left_p_h, right_q_h, left_b_h, twist_h, column_h, pool_h,
    out,
    x, s, r, cs, ang, foc, gat0, gat1, gat2, cross, osend, orecv,
    fil_raw, fil, left_p_f, right_q_f, left_b_f, left_p, right_q, left_b, left_k, twist, column, pool,
    in_sem, turn_send, turn_recv, turn_own, acq_send, acq_recv, acq_own, out_send, out_recv, out_own,
):
    me_a, me_t = lax.axis_index("acq"), lax.axis_index("tile")
    gat = (gat0, gat1, gat2)

    early = [
        pltpu.make_async_copy(left_p_h, left_p_f, in_sem.at[0]),
        pltpu.make_async_copy(right_q_h, right_q_f, in_sem.at[1]),
        pltpu.make_async_copy(filt, fil_raw, in_sem.at[2]),
        pltpu.make_async_copy(echo, x, in_sem.at[3]),
        pltpu.make_async_copy(twist_h, twist, in_sem.at[4]),
    ]
    late = [
        *[
            pltpu.make_async_copy(angle.at[:, pl.ds(128 * j, 128)], ang.at[j], in_sem.at[10 + j])
            for j in range(CHUNKS)
        ],
        pltpu.make_async_copy(left_b_h, left_b_f, in_sem.at[7]),
        pltpu.make_async_copy(column_h, column, in_sem.at[8]),
        pltpu.make_async_copy(pool_h, pool, in_sem.at[9]),
    ]
    for copy in early + late:
        copy.start()

    barrier = pltpu.get_barrier_semaphore()

    def greet_tile(k, _):
        peer = lax.rem(me_t + k, TILE)
        pl.semaphore_signal(barrier, inc=1, device_id={"tile": peer}, device_id_type=MESH)
        return 0

    def greet_acq(k, _):
        peer = lax.rem(me_a + k, ACQ)
        pl.semaphore_signal(barrier, inc=1, device_id={"acq": peer}, device_id_type=MESH)
        return 0

    def greet_source(k, _):
        source_a = me_t // 4

        @pl.when(jnp.logical_or(source_a != me_a, k != me_t))
        def _():
            pl.semaphore_signal(
                barrier, inc=1, device_id={"acq": source_a, "tile": k}, device_id_type=MESH
            )

        return 0

    lax.fori_loop(1, TILE, greet_tile, 0)
    lax.fori_loop(1, ACQ, greet_acq, 0)
    lax.fori_loop(0, TILE, greet_source, 0)
    early[0].wait()
    left_p[...] = left_p_f[...].astype(jnp.bfloat16)
    early[1].wait()
    high, low = halves(right_q_f[...])
    right_q[...] = jnp.concatenate([high, high, low], axis=0)
    early[2].wait()
    for c in range(2):
        fil[c] = fil_raw[c].T
    early[3].wait()
    early[4].wait()

    def compress(g):
        for part in range(2):
            ids = range(4 * part, 4 * part + 4)
            value = jnp.concatenate(
                [
                    jnp.concatenate([x[c, (3 * i + g) // 8, pl.ds((3 * i + g) % 8, NP, stride=8), :] for i in ids], axis=1)
                    for c in range(2)
                ],
                axis=0,
            )
            value = left_product(left_p[...], value)
            tr, ti = twist[0], twist[1]
            rows = []
            for n in range(4):
                re = value[:NP, n * NQ : (n + 1) * NQ]
                im = value[NP:, n * NQ : (n + 1) * NQ]
                rows.append(jnp.concatenate([re * tr - im * ti, re * ti + im * tr], axis=1))
            value = right_product(jnp.concatenate(rows, axis=0), right_q[...])
            fr, fi = fil[0], fil[1]
            rows = []
            for n in range(4):
                re = value[n * NP : (n + 1) * NP, :NQ]
                im = value[n * NP : (n + 1) * NP, NQ:]
                rows.append(jnp.concatenate([re * fi + im * fr, re * fr - im * fi], axis=1))
            value = right_product(jnp.concatenate(rows, axis=0), right_q[...])
            top, low = [], []
            for n in range(4):
                im = value[n * NP : (n + 1) * NP, :NQ]
                re = value[n * NP : (n + 1) * NP, NQ:]
                top.append(im * tr - re * ti)
                low.append(re * tr + im * ti)
            value = jnp.concatenate(
                [jnp.concatenate(top, axis=1), jnp.concatenate(low, axis=1)], axis=0
            )
            value = left_product(left_p[...], value)
            for n, i in enumerate(ids):
                s[g, 1, pl.ds(i, NP, stride=8), :] = value[:NP, n * NQ : (n + 1) * NQ]
                s[g, 0, pl.ds(i, NP, stride=8), :] = value[NP:, n * NQ : (n + 1) * NQ]

    def turn(j, groups):
        def send(k, _):
            peer = lax.rem(me_t + k, TILE)
            pltpu.make_async_remote_copy(
                src_ref=s.at[groups, :, pl.ds((CHUNKS * peer + j) * 8, 8), :],
                dst_ref=r.at[j, groups, :, pl.ds(me_t * 8, 8), :],
                send_sem=turn_send.at[j],
                recv_sem=turn_recv.at[j],
                device_id={"tile": peer},
                device_id_type=MESH,
            ).start()
            return 0

        lax.fori_loop(1, TILE, send, 0)

    def own_turn(j):
        return pltpu.make_async_copy(
            s.at[:, :, pl.ds((CHUNKS * me_t + j) * 8, 8), :],
            r.at[j, :, :, pl.ds(me_t * 8, 8), :],
            turn_own.at[j],
        )

    for g in range(GROUPS):
        compress(g)
        if g == 0:
            own_is_dest = (me_t // 4 == me_a).astype(jnp.int32)
            pl.semaphore_wait(barrier, (TILE - 1) + (ACQ - 1) + DESTS - own_is_dest)
        turn(0, pl.ds(g, 1))
    for j in range(1, CHUNKS):
        turn(j, pl.ds(0, GROUPS))
    for j in range(CHUNKS):
        own_turn(j).start()
    for copy in late:
        copy.wait()
    high, low = halves(left_b_f[...])
    left_b[...] = jnp.concatenate([high, high, low], axis=1)
    kept = jnp.concatenate(
        [left_b_f[FIRST : FIRST + KEPT, :], left_b_f[NB + FIRST : NB + FIRST + KEPT, :]], axis=0
    )
    high, low = halves(kept)
    left_k[...] = jnp.concatenate([high, high, low], axis=1)

    def phases(j):
        for h in range(12):
            rows = pl.ds(h * 64, 64)
            a = ang[j, rows, :]
            cs[j, 0, rows, :] = jnp.cos(a) * (1.0 / NA / NR)
            cs[j, 1, rows, :] = jnp.sin(a) * (1.0 / NA / NR)

    root = float(np.sqrt(0.75))

    def butterfly(re, im, sign):
        sr, si = re[1] + re[2], im[1] + im[2]
        dr, di = (re[1] - re[2]) * (sign * root), (im[1] - im[2]) * (sign * root)
        mr, mi = re[0] - 0.5 * sr, im[0] - 0.5 * si
        return [re[0] + sr, mr - di, mr + di], [im[0] + si, mi + dr, mi - dr]

    def focus(j):
        value = jnp.concatenate(
            [jnp.concatenate([r[j, a, c] for a in range(3)], axis=1) for c in range(2)], axis=0
        )
        value = left_product(left_b[...], value)
        re = [value[:NB, a * 128 : (a + 1) * 128] for a in range(3)]
        im = [value[NB:, a * 128 : (a + 1) * 128] for a in range(3)]
        for a in (1, 2):
            tr, ti = column[:, 2 * a - 2 : 2 * a - 1], column[:, 2 * a - 1 : 2 * a]
            re[a], im[a] = re[a] * tr - im[a] * ti, re[a] * ti + im[a] * tr
        re, im = butterfly(re, im, -1.0)
        for f1 in range(3):
            c, d = cs[j, 0, f1 * NB : (f1 + 1) * NB, :], cs[j, 1, f1 * NB : (f1 + 1) * NB, :]
            re[f1], im[f1] = re[f1] * c - im[f1] * d, re[f1] * d + im[f1] * c
        re, im = butterfly(re, im, 1.0)
        for a in (1, 2):
            tr, ti = column[:, 2 * a - 2 : 2 * a - 1], column[:, 2 * a - 1 : 2 * a]
            re[a], im[a] = re[a] * tr + im[a] * ti, im[a] * tr - re[a] * ti
        value = jnp.concatenate([jnp.concatenate(im, axis=1), jnp.concatenate(re, axis=1)], axis=0)
        value = left_product(left_k[...], value)
        for a in range(3):
            rows = pl.ds(8 + 3 * FIRST + a - AOI_START, 86, stride=3)
            foc[j, 1, rows, :] = value[:86, a * 128 : (a + 1) * 128]
            foc[j, 0, rows, :] = value[KEPT : KEPT + 86, a * 128 : (a + 1) * 128]

    def own_share(j):
        return pltpu.make_async_copy(
            foc.at[j, :, pl.ds(8 + me_a * PART, PART), :], gat[j].at[me_a], acq_own.at[j]
        )

    def share(j):
        def send(k, _):
            peer = lax.rem(me_a + k, ACQ)
            pltpu.make_async_remote_copy(
                src_ref=foc.at[j, :, pl.ds(8 + peer * PART, PART), :],
                dst_ref=gat[j].at[me_a],
                send_sem=acq_send.at[j],
                recv_sem=acq_recv.at[j],
                device_id={"acq": peer},
                device_id_type=MESH,
            ).start()
            return 0

        lax.fori_loop(1, ACQ, send, 0)
        own_share(j).start()

    def take_share(j):
        whole = gat[j].at[pl.ds(0, ACQ - 1)]
        pltpu.make_async_copy(whole, whole, acq_recv.at[j]).wait()
        own_share(j).wait()

    def interfere(j):
        def one(a, _):
            mine = [[gat[j][a, c, pl.ds(o, 16, stride=2), :] for o in (0, 1)] for c in range(2)]
            for round_id in range(2):
                b = pairs[round_id, a]
                other = [[gat[j][b, c, pl.ds(o, 16, stride=2), :] for o in (0, 1)] for c in range(2)]
                re = sum(mine[c][o] * other[c][o] for c in range(2) for o in range(2))
                im = sum(mine[1][o] * other[0][o] - mine[0][o] * other[1][o] for o in range(2))
                for i in range(4):
                    cross[0, a, i, 4 * round_id : 4 * round_id + 4, :] = re[4 * i : 4 * i + 4]
                    cross[1, a, i, 4 * round_id : 4 * round_id + 4, :] = im[4 * i : 4 * i + 4]
            return 0

        lax.fori_loop(0, ACQ, one, 0)
        re_high, re_low = halves(cross[0].reshape(DESTS * 8, 128))
        im_high, im_low = halves(cross[1].reshape(DESTS * 8, 128))
        lhs = jnp.concatenate([re_high, im_high, re_low, im_low], axis=1)
        sums = pool[j].astype(jnp.bfloat16)
        sums = jnp.concatenate([sums, sums], axis=0)
        looked = jnp.dot(lhs, sums, preferred_element_type=jnp.float32)
        if j == 0:
            osend[...] = looked
        else:
            osend[...] += looked

    phases(0)
    for j in range(CHUNKS):
        if j + 1 < CHUNKS:
            phases(j + 1)
        own_turn(j).wait()
        whole = r.at[j, :, :, pl.ds(0, (TILE - 1) * 8), :]
        pltpu.make_async_copy(whole, whole, turn_recv.at[j]).wait()
        focus(j)
        share(j)
        if j:
            take_share(j - 1)
            interfere(j - 1)
    take_share(CHUNKS - 1)
    interfere(CHUNKS - 1)

    def send_out(d, _):
        dest_a, dest_t = d // 4, 4 * me_a + lax.rem(d, 4)
        own = jnp.logical_and(dest_a == me_a, dest_t == me_t)

        @pl.when(jnp.logical_not(own))
        def _():
            pltpu.make_async_remote_copy(
                src_ref=osend.at[pl.ds(8 * d, 8), :],
                dst_ref=orecv.at[pl.ds(8 * me_t, 8), :],
                send_sem=out_send,
                recv_sem=out_recv,
                device_id={"acq": dest_a, "tile": dest_t},
                device_id_type=MESH,
            ).start()

        return 0

    lax.fori_loop(0, DESTS, send_out, 0)
    has_own = me_t // 4 == me_a

    def out_wait(sem, count):
        whole = orecv.at[pl.ds(0, 8 * count), :]
        pltpu.make_async_copy(whole, whole, sem).wait()

    @pl.when(has_own)
    def _():
        d = 4 * me_a + lax.rem(me_t, 4)
        copy = pltpu.make_async_copy(
            osend.at[pl.ds(8 * d, 8), :], orecv.at[pl.ds(8 * me_t, 8), :], out_own
        )
        copy.start()
        copy.wait()
        out_wait(out_recv, DESTS - 1)
        out_wait(out_send, DESTS - 1)

    @pl.when(jnp.logical_not(has_own))
    def _():
        out_wait(out_recv, DESTS)
        out_wait(out_send, DESTS)

    lane = lax.broadcasted_iota(jnp.int32, (8, 128), 1)
    for c in range(2):
        for v in range(12):
            total = jnp.zeros((8, 128), jnp.float32)
            for t in range((128 * v) // 48, (128 * v + 127) // 48 + 1):
                start = 48 * t - 128 * v
                moved = pltpu.roll(orecv[8 * t : 8 * t + 8, :], (start - 64 * c) % 128, 1)
                inside = jnp.logical_and(lane >= start, lane < start + 48)
                total = jnp.where(inside, moved, total)
            for round_id in range(2):
                out[c, round_id, 0, :, 128 * v : 128 * (v + 1)] = total[4 * round_id : 4 * round_id + 4]

    for j in range(CHUNKS):
        whole = r.at[j, :, :, pl.ds(0, (TILE - 1) * 8), :]
        pltpu.make_async_copy(whole, whole, turn_send.at[j]).wait()
        whole = gat[j].at[pl.ds(0, ACQ - 1)]
        pltpu.make_async_copy(whole, whole, acq_send.at[j]).wait()


def shards(unprocessed_echo_data, slant_kernel_frequencies, along_track_kernel_angle, pairs):
    echo = unprocessed_echo_data.reshape(2, GROUPS, 8, NP, NQ)
    echo = echo.transpose(0, 1, 3, 2, 4).reshape(2, GROUPS, NP * 8, NQ)
    filt = slant_kernel_frequencies.reshape(2, NQ, NP)
    angle = along_track_kernel_angle[0]
    consts = [jnp.asarray(t) for t in tables()]
    any_spec = pl.BlockSpec(memory_space=pl.ANY)
    f32 = jnp.float32
    vmem, dma = pltpu.VMEM, pltpu.SemaphoreType.DMA
    return pl.pallas_call(
        kernel,
        out_shape=jax.ShapeDtypeStruct((2, 2, 1, 4, NR // 8), f32),
        in_specs=[pl.BlockSpec(memory_space=pltpu.SMEM)] + [any_spec] * 9,
        out_specs=pl.BlockSpec(memory_space=pltpu.VMEM),
        scratch_shapes=[
            vmem((2, GROUPS, NP * 8, NQ), f32),
            vmem((GROUPS, 2, NP * 8, NQ), f32),
            vmem((CHUNKS, GROUPS, 2, NB, 128), f32),
            vmem((CHUNKS, 2, NA, 128), f32),
            vmem((CHUNKS, NA, 128), f32),
            vmem((CHUNKS, 2, AOI + 16, 128), f32),
            vmem((ACQ, 2, PART, 128), f32),
            vmem((ACQ, 2, PART, 128), f32),
            vmem((ACQ, 2, PART, 128), f32),
            vmem((2, ACQ, 4, 8, 128), f32),
            vmem((DESTS * 8, 128), f32),
            vmem((DESTS * 8, 128), f32),
            vmem((2, NQ, NP), f32),
            vmem((2, NP, NQ), f32),
            vmem((2 * NP, 6 * NP), f32),
            vmem((2 * NQ, 2 * NQ), f32),
            vmem((2 * NB, 2 * NB), f32),
            vmem((2 * NP, 6 * NP), jnp.bfloat16),
            vmem((6 * NQ, 2 * NQ), jnp.bfloat16),
            vmem((2 * NB, 6 * NB), jnp.bfloat16),
            vmem((2 * KEPT, 6 * NB), jnp.bfloat16),
            vmem((2, NP, NQ), f32),
            vmem((NB, 128), f32),
            vmem((CHUNKS, 2 * 128, 128), f32),
            dma((13,)),
            dma((CHUNKS,)),
            dma((CHUNKS,)),
            dma((CHUNKS,)),
            dma((CHUNKS,)),
            dma((CHUNKS,)),
            dma((CHUNKS,)),
            dma,
            dma,
            dma,
        ],
        name="range_doppler",
        compiler_params=pltpu.CompilerParams(
            collective_id=0, has_side_effects=True, vmem_limit_bytes=56 * 2**20
        ),
    )(pairs, echo, filt, angle, *consts)


def solution(mesh):
    in_specs = (P(None, "acq", "tile", None), P(None, "acq", None), P("acq", None, "tile"), P())
    out_specs = P(None, None, "acq", "tile", None)
    return jax.shard_map(shards, mesh=mesh, in_specs=in_specs, out_specs=out_specs, check_vma=False)
```

```python
import jax
import jax.numpy as jnp
import ml_dtypes
import numpy as np
from jax import lax
from jax.experimental import pallas as pl
from jax.experimental.pallas import tpu as pltpu
from jax.sharding import PartitionSpec as P

MESH = pl.DeviceIdType.MESH
NA, NR, AOI, AOI_START = 768, 12288, 256, 256
NP, NQ = 96, 128
NB = 256
ACQ, TILE = 8, 32
GROUPS = 3
CHUNKS = 3
FIRST = AOI_START // 3
KEPT = 88
PART = AOI // ACQ
DESTS = TILE


def split3(matrix):
    high = matrix.astype(ml_dtypes.bfloat16)
    low = (matrix - high.astype(np.float64)).astype(ml_dtypes.bfloat16)
    return np.concatenate([high, high, low], axis=1).astype(np.float32)


def dft_block(size):
    ids = np.arange(size)
    angle = 2.0 * np.pi * (np.outer(ids, ids) % size) / size
    c, s = np.cos(angle), np.sin(angle)
    return np.block([[c, s], [-s, c]])


def tables():
    left_p = split3(dft_block(NP))
    right_q = dft_block(NQ).T.astype(np.float32)
    left_b = dft_block(NB).astype(np.float32)
    angle = 2.0 * np.pi * np.outer(np.arange(NP), np.arange(NQ)) / NR
    twist = np.stack([np.cos(angle), -np.sin(angle)]).astype(np.float32)
    column = np.zeros((NB, 128), np.float64)
    ids = np.arange(NB)
    for a in (1, 2):
        column[:, 2 * a - 2] = np.cos(2.0 * np.pi * a * ids / NA)
        column[:, 2 * a - 1] = -np.sin(2.0 * np.pi * a * ids / NA)
    return left_p, right_q, left_b, twist, column.astype(np.float32)


def halves(value):
    high = value.astype(jnp.bfloat16)
    return high, (value - high.astype(jnp.float32)).astype(jnp.bfloat16)


def left_product(table, value):
    high, low = halves(value)
    rhs = jnp.concatenate([high, low, high], axis=0)
    return jnp.dot(table, rhs, preferred_element_type=jnp.float32)


def right_product(value, table):
    high, low = halves(value)
    lhs = jnp.concatenate([high, low, high], axis=1)
    return jnp.dot(lhs, table, preferred_element_type=jnp.float32)


def kernel(
    pairs, echo, filt, angle, left_p_h, right_q_h, left_b_h, twist_h, column_h,
    out,
    x, s, r, cs, ang, foc, gat0, gat1, gat2, sides, osend, orecv,
    fil_raw, fil_turn, fil, left_p_f, right_q_f, left_b_f, left_p, right_q, left_b, left_k, twist, column, pool, place,
    in_sem, turn_send, turn_recv, turn_own, acq_send, acq_recv, acq_own, out_send, out_recv, out_own,
):
    me_a, me_t = lax.axis_index("acq"), lax.axis_index("tile")
    gat = (gat0, gat1, gat2)

    early = [
        pltpu.make_async_copy(left_p_h, left_p_f, in_sem.at[0]),
        pltpu.make_async_copy(right_q_h, right_q_f, in_sem.at[1]),
        pltpu.make_async_copy(filt, fil_raw, in_sem.at[2]),
        pltpu.make_async_copy(twist_h, twist, in_sem.at[3]),
    ]
    lines = [pltpu.make_async_copy(echo.at[:, i], x.at[:, i], in_sem.at[4 + i]) for i in range(3)]
    late = [
        *[
            pltpu.make_async_copy(angle.at[:, pl.ds(128 * j, 128)], ang.at[j], in_sem.at[9 + j])
            for j in range(CHUNKS)
        ],
        pltpu.make_async_copy(left_b_h, left_b_f, in_sem.at[7]),
        pltpu.make_async_copy(column_h, column, in_sem.at[8]),
    ]
    for copy in early[:2] + lines[:2] + early[2:] + lines[2:] + late:
        copy.start()

    barrier = pltpu.get_barrier_semaphore()

    def greet_tile(k, _):
        peer = lax.rem(me_t + k, TILE)
        pl.semaphore_signal(barrier, inc=1, device_id={"tile": peer}, device_id_type=MESH)
        return 0

    def greet_acq(k, _):
        peer = lax.rem(me_a + k, ACQ)
        pl.semaphore_signal(barrier, inc=1, device_id={"acq": peer}, device_id_type=MESH)
        return 0

    def greet_source(k, _):
        source_a = me_t // 4

        @pl.when(jnp.logical_or(source_a != me_a, k != me_t))
        def _():
            pl.semaphore_signal(
                barrier, inc=1, device_id={"acq": source_a, "tile": k}, device_id_type=MESH
            )

        return 0

    lax.fori_loop(1, TILE, greet_tile, 0)
    lax.fori_loop(1, ACQ, greet_acq, 0)
    lax.fori_loop(0, TILE, greet_source, 0)
    early[0].wait()
    left_p[...] = left_p_f[...].astype(jnp.bfloat16)
    early[1].wait()
    high, low = halves(right_q_f[...])
    right_q[...] = jnp.concatenate([high, high, low], axis=0)
    early[2].wait()
    lane = lax.broadcasted_iota(jnp.int32, (32, 128), 1)
    for c in range(2):
        v = [fil_raw[c, pl.ds(w, 32, stride=3), :] for w in range(3)]
        fil_turn[pl.ds(0, 32, stride=4), :] = v[0]
        fil_turn[pl.ds(1, 32, stride=4), :] = jnp.where(
            lane < 32, pltpu.roll(v[0], 32, 1), pltpu.roll(v[1], 32, 1)
        )
        fil_turn[pl.ds(2, 32, stride=4), :] = jnp.where(
            lane < 64, pltpu.roll(v[1], 64, 1), pltpu.roll(v[2], 64, 1)
        )
        fil_turn[pl.ds(3, 32, stride=4), :] = pltpu.roll(v[2], 96, 1)
        fil[c] = fil_turn[...].T[:NP]
    early[3].wait()
    lines[0].wait()
    lines[1].wait()

    def compress(g):
        for part in range(2):
            if g == 0 and part == 1:
                lines[2].wait()
            ids = range(4 * part, 4 * part + 4)
            value = jnp.concatenate(
                [
                    jnp.concatenate([x[c, (3 * i + g) // 8, pl.ds((3 * i + g) % 8, NP, stride=8), :] for i in ids], axis=1)
                    for c in range(2)
                ],
                axis=0,
            )
            value = left_product(left_p[...], value)
            tr, ti = twist[0], twist[1]
            rows = []
            for n in range(4):
                re = value[:NP, n * NQ : (n + 1) * NQ]
                im = value[NP:, n * NQ : (n + 1) * NQ]
                rows.append(jnp.concatenate([re * tr - im * ti, re * ti + im * tr], axis=1))
            value = right_product(jnp.concatenate(rows, axis=0), right_q[...])
            fr, fi = fil[0], fil[1]
            rows = []
            for n in range(4):
                re = value[n * NP : (n + 1) * NP, :NQ]
                im = value[n * NP : (n + 1) * NP, NQ:]
                rows.append(jnp.concatenate([re * fi + im * fr, re * fr - im * fi], axis=1))
            value = right_product(jnp.concatenate(rows, axis=0), right_q[...])
            top, low = [], []
            for n in range(4):
                im = value[n * NP : (n + 1) * NP, :NQ]
                re = value[n * NP : (n + 1) * NP, NQ:]
                top.append(im * tr - re * ti)
                low.append(re * tr + im * ti)
            value = jnp.concatenate(
                [jnp.concatenate(top, axis=1), jnp.concatenate(low, axis=1)], axis=0
            )
            value = left_product(left_p[...], value)
            for n, i in enumerate(ids):
                s[g, 1, pl.ds(i, NP, stride=8), :] = value[:NP, n * NQ : (n + 1) * NQ]
                s[g, 0, pl.ds(i, NP, stride=8), :] = value[NP:, n * NQ : (n + 1) * NQ]

    def turn(j, groups, sem):
        def send(k, _):
            peer = lax.rem(me_t + k, TILE)
            pltpu.make_async_remote_copy(
                src_ref=s.at[groups, :, pl.ds((CHUNKS * peer + j) * 8, 8), :],
                dst_ref=r.at[j, groups, :, pl.ds(me_t * 8, 8), :],
                send_sem=turn_send.at[j, sem],
                recv_sem=turn_recv.at[j, sem],
                device_id={"tile": peer},
                device_id_type=MESH,
            ).start()
            return 0

        lax.fori_loop(1, TILE, send, 0)

    def turn_wait(j, sems, g=None):
        if j == 1:
            whole = r.at[j, :, :, pl.ds(0, (TILE - 1) * 8), :]
            pltpu.make_async_copy(whole, whole, sems.at[j, 0]).wait()
        else:
            for i in range(GROUPS) if g is None else (g,):
                whole = r.at[j, i, :, pl.ds(0, (TILE - 1) * 8), :]
                pltpu.make_async_copy(whole, whole, sems.at[j, i]).wait()

    def own_turn(j):
        return pltpu.make_async_copy(
            s.at[:, :, pl.ds((CHUNKS * me_t + j) * 8, 8), :],
            r.at[j, :, :, pl.ds(me_t * 8, 8), :],
            turn_own.at[j],
        )

    for g in range(GROUPS):
        compress(g)
        if g == 0:
            own_is_dest = (me_t // 4 == me_a).astype(jnp.int32)
            pl.semaphore_wait(barrier, (TILE - 1) + (ACQ - 1) + DESTS - own_is_dest)
        turn(0, pl.ds(g, 1), g)
    turn(1, pl.ds(0, GROUPS), 0)
    for g in range(GROUPS):
        turn(2, pl.ds(g, 1), g)
    for j in range(CHUNKS):
        own_turn(j).start()
    for copy in late:
        copy.wait()
    high, low = halves(left_b_f[...])
    left_b[...] = jnp.concatenate([high, high, low], axis=1)
    kept = jnp.concatenate(
        [left_b_f[FIRST : FIRST + KEPT, :], left_b_f[NB + FIRST : NB + FIRST + KEPT, :]], axis=0
    )
    high, low = halves(kept)
    left_k[...] = jnp.concatenate([high, high, low], axis=1)
    row = lax.broadcasted_iota(jnp.int32, (1024, 128), 0)
    col = lax.broadcasted_iota(jnp.int32, (1024, 128), 1)
    same = jnp.logical_and(col // 16 == row // 128, col % 16 == row % 128 // 8)
    value = jnp.where(same, 1.0 / 16.0, 0.0).astype(jnp.bfloat16)
    pool[...] = jnp.concatenate([value, value], axis=0)
    same = jnp.logical_and(col // 16 == row // 128, col % 16 == row % 16)
    value = jnp.where(same, 1.0, 0.0).astype(jnp.bfloat16)
    place[...] = jnp.concatenate([value, value], axis=0)

    def phases(j):
        for h in range(12):
            rows = pl.ds(h * 64, 64)
            a = ang[j, rows, :]
            cs[j, 0, rows, :] = jnp.cos(a) * (1.0 / NA / NR)
            cs[j, 1, rows, :] = jnp.sin(a) * (1.0 / NA / NR)

    root = float(np.sqrt(0.75))

    def butterfly(re, im, sign):
        sr, si = re[1] + re[2], im[1] + im[2]
        dr, di = (re[1] - re[2]) * (sign * root), (im[1] - im[2]) * (sign * root)
        mr, mi = re[0] - 0.5 * sr, im[0] - 0.5 * si
        return [re[0] + sr, mr - di, mr + di], [im[0] + si, mi + dr, mi - dr]

    def focus(j):
        if j < CHUNKS - 1:
            turn_wait(j, turn_recv)
            value = jnp.concatenate(
                [jnp.concatenate([r[j, a, c] for a in range(3)], axis=1) for c in range(2)], axis=0
            )
            value = left_product(left_b[...], value)
            re = [value[:NB, a * 128 : (a + 1) * 128] for a in range(3)]
            im = [value[NB:, a * 128 : (a + 1) * 128] for a in range(3)]
        else:
            re, im = [], []
            for a in range(3):
                turn_wait(j, turn_recv, a)
                value = left_product(left_b[...], jnp.concatenate([r[j, a, 0], r[j, a, 1]], axis=0))
                re.append(value[:NB])
                im.append(value[NB:])
        for a in (1, 2):
            tr, ti = column[:, 2 * a - 2 : 2 * a - 1], column[:, 2 * a - 1 : 2 * a]
            re[a], im[a] = re[a] * tr - im[a] * ti, re[a] * ti + im[a] * tr
        re, im = butterfly(re, im, -1.0)
        for f1 in range(3):
            c, d = cs[j, 0, f1 * NB : (f1 + 1) * NB, :], cs[j, 1, f1 * NB : (f1 + 1) * NB, :]
            re[f1], im[f1] = re[f1] * c - im[f1] * d, re[f1] * d + im[f1] * c
        re, im = butterfly(re, im, 1.0)
        for a in (1, 2):
            tr, ti = column[:, 2 * a - 2 : 2 * a - 1], column[:, 2 * a - 1 : 2 * a]
            re[a], im[a] = re[a] * tr + im[a] * ti, im[a] * tr - re[a] * ti
        value = jnp.concatenate([jnp.concatenate(im, axis=1), jnp.concatenate(re, axis=1)], axis=0)
        value = left_product(left_k[...], value)
        for a in range(3):
            rows = pl.ds(8 + 3 * FIRST + a - AOI_START, 86, stride=3)
            foc[j, 1, rows, :] = value[:86, a * 128 : (a + 1) * 128]
            foc[j, 0, rows, :] = value[KEPT : KEPT + 86, a * 128 : (a + 1) * 128]

    def own_share(j):
        return pltpu.make_async_copy(
            foc.at[j, :, pl.ds(8 + me_a * PART, PART), :], gat[j].at[me_a], acq_own.at[j]
        )

    def share(j):
        def send(k, _):
            peer = lax.rem(me_a + k, ACQ)
            pltpu.make_async_remote_copy(
                src_ref=foc.at[j, :, pl.ds(8 + peer * PART, PART), :],
                dst_ref=gat[j].at[me_a],
                send_sem=acq_send.at[j],
                recv_sem=acq_recv.at[j],
                device_id={"acq": peer},
                device_id_type=MESH,
            ).start()
            return 0

        lax.fori_loop(1, ACQ, send, 0)
        own_share(j).start()

    def take_share(j):
        whole = gat[j].at[pl.ds(0, ACQ - 1)]
        pltpu.make_async_copy(whole, whole, acq_recv.at[j]).wait()
        own_share(j).wait()

    def interfere(j):
        def line_up(a, _):
            rows = pl.ds(pl.multiple_of(a * PART, PART), PART)
            for c in range(2):
                sides[2, c, rows, :] = gat[j][a, c]
                for round_id in range(2):
                    sides[round_id, c, rows, :] = gat[j][pairs[round_id, a], c]
            return 0

        lax.fori_loop(0, ACQ, line_up, 0)
        re, im = [], []
        for round_id in range(2):
            for l in range(4):
                sum_re, sum_im = 0.0, 0.0
                for o in range(2):
                    rows = pl.ds(2 * l + o, DESTS, stride=8)
                    mr, mi = sides[2, 0, rows, :], sides[2, 1, rows, :]
                    pr, pi = sides[round_id, 0, rows, :], sides[round_id, 1, rows, :]
                    sum_re += mr * pr + mi * pi
                    sum_im += mi * pr - mr * pi
                re.append(sum_re)
                im.append(sum_im)
        value = jnp.concatenate([jnp.concatenate(re, axis=1), jnp.concatenate(im, axis=1)], axis=0)
        looked = jnp.dot(
            jnp.concatenate(halves(value), axis=1), pool[...], preferred_element_type=jnp.float32
        )
        for c in range(2):
            osend[j, c] = looked[c * DESTS : (c + 1) * DESTS].reshape(DESTS, 1, 128)

    has_own = me_t // 4 == me_a

    def send_out(j):
        def send(d, _):
            dest_a, dest_t = d // 4, 4 * me_a + lax.rem(d, 4)
            own = jnp.logical_and(dest_a == me_a, dest_t == me_t)

            @pl.when(jnp.logical_not(own))
            def _():
                pltpu.make_async_remote_copy(
                    src_ref=osend.at[j, :, d],
                    dst_ref=orecv.at[j, :, me_t],
                    send_sem=out_send.at[j],
                    recv_sem=out_recv.at[j],
                    device_id={"acq": dest_a, "tile": dest_t},
                    device_id_type=MESH,
                ).start()

            return 0

        lax.fori_loop(0, DESTS, send, 0)

        @pl.when(has_own)
        def _():
            own_out(j).start()

    def own_out(j):
        return pltpu.make_async_copy(
            osend.at[j, :, 4 * me_a + lax.rem(me_t, 4)], orecv.at[j, :, me_t], out_own.at[j]
        )

    def out_wait(j, sem):
        def wait(count):
            whole = orecv.at[j, :, pl.ds(0, count)]
            pltpu.make_async_copy(whole, whole, sem).wait()

        @pl.when(has_own)
        def _():
            wait(DESTS - 1)

        @pl.when(jnp.logical_not(has_own))
        def _():
            wait(DESTS)

    phases(0)
    for j in range(CHUNKS):
        if j + 1 < CHUNKS:
            phases(j + 1)
        own_turn(j).wait()
        focus(j)
        share(j)
        if j:
            take_share(j - 1)
            interfere(j - 1)
            send_out(j - 1)
    take_share(CHUNKS - 1)
    interfere(CHUNKS - 1)
    send_out(CHUNKS - 1)
    for j in range(CHUNKS):
        turn_wait(j, turn_send)
        whole = gat[j].at[pl.ds(0, ACQ - 1)]
        pltpu.make_async_copy(whole, whole, acq_send.at[j]).wait()
        out_wait(j, out_send.at[j])
    for j in range(CHUNKS):
        out_wait(j, out_recv.at[j])

        @pl.when(has_own)
        def _():
            own_out(j).wait()

    which = lax.broadcasted_iota(jnp.int32, (8, 128), 0)
    mask = lax.broadcasted_iota(jnp.int32, (8, 128), 1) // 16 == which
    blocks = []
    for c in range(2):
        for v in range(12):
            pieces = [(u // CHUNKS, u % CHUNKS) for u in range(8 * v, 8 * v + 8)]
            spread = [jnp.where(mask, orecv[j, c, t], 0.0) for t, j in pieces]
            blocks.append(jnp.concatenate(spread, axis=1))
    value = jnp.concatenate(blocks, axis=0)
    value = jnp.dot(
        jnp.concatenate(halves(value), axis=1), place[...], preferred_element_type=jnp.float32
    )
    for c in range(2):
        for v in range(12):
            for round_id in range(2):
                first = (c * 12 + v) * 8 + 4 * round_id
                out[c, round_id, v] = value[first : first + 4]


def shards(unprocessed_echo_data, slant_kernel_frequencies, along_track_kernel_angle, pairs):
    echo = unprocessed_echo_data.reshape(2, GROUPS, 8, NP, NQ)
    echo = echo.transpose(0, 1, 3, 2, 4).reshape(2, GROUPS, NP * 8, NQ)
    filt = slant_kernel_frequencies.reshape(2, NP, NQ)
    angle = along_track_kernel_angle[0]
    consts = [jnp.asarray(t) for t in tables()]
    any_spec = pl.BlockSpec(memory_space=pl.ANY)
    f32 = jnp.float32
    vmem, dma = pltpu.VMEM, pltpu.SemaphoreType.DMA
    blocks = pl.pallas_call(
        kernel,
        out_shape=jax.ShapeDtypeStruct((2, 2, 12, 4, 128), f32),
        in_specs=[pl.BlockSpec(memory_space=pltpu.SMEM)] + [any_spec] * 8,
        out_specs=pl.BlockSpec(memory_space=pltpu.VMEM),
        scratch_shapes=[
            vmem((2, GROUPS, NP * 8, NQ), f32),
            vmem((GROUPS, 2, NP * 8, NQ), f32),
            vmem((CHUNKS, GROUPS, 2, NB, 128), f32),
            vmem((CHUNKS, 2, NA, 128), f32),
            vmem((CHUNKS, NA, 128), f32),
            vmem((CHUNKS, 2, AOI + 16, 128), f32),
            vmem((ACQ, 2, PART, 128), f32),
            vmem((ACQ, 2, PART, 128), f32),
            vmem((ACQ, 2, PART, 128), f32),
            vmem((3, 2, ACQ * PART, 128), f32),
            vmem((CHUNKS, 2, DESTS, 1, 128), f32),
            vmem((CHUNKS, 2, DESTS, 1, 128), f32),
            vmem((2, NP, NQ), f32),
            vmem((NQ, 128), f32),
            vmem((2, NP, NQ), f32),
            vmem((2 * NP, 6 * NP), f32),
            vmem((2 * NQ, 2 * NQ), f32),
            vmem((2 * NB, 2 * NB), f32),
            vmem((2 * NP, 6 * NP), jnp.bfloat16),
            vmem((6 * NQ, 2 * NQ), jnp.bfloat16),
            vmem((2 * NB, 6 * NB), jnp.bfloat16),
            vmem((2 * KEPT, 6 * NB), jnp.bfloat16),
            vmem((2, NP, NQ), f32),
            vmem((NB, 128), f32),
            vmem((2 * 8 * 128, 128), jnp.bfloat16),
            vmem((2 * 8 * 128, 128), jnp.bfloat16),
            dma((12,)),
            dma((CHUNKS, GROUPS)),
            dma((CHUNKS, GROUPS)),
            dma((CHUNKS,)),
            dma((CHUNKS,)),
            dma((CHUNKS,)),
            dma((CHUNKS,)),
            dma((CHUNKS,)),
            dma((CHUNKS,)),
            dma((CHUNKS,)),
        ],
        name="range_doppler",
        compiler_params=pltpu.CompilerParams(
            collective_id=0, has_side_effects=True, vmem_limit_bytes=56 * 2**20
        ),
    )(pairs, echo, filt, angle, *consts)
    return blocks.transpose(0, 1, 3, 2, 4).reshape(2, 2, 1, 4, NR // 8)


def solution(mesh):
    in_specs = (P(None, "acq", "tile", None), P(None, "acq", None), P("acq", None, "tile"), P())
    out_specs = P(None, None, "acq", "tile", None)
    return jax.shard_map(shards, mesh=mesh, in_specs=in_specs, out_specs=out_specs, check_vma=False)
```

```python
import jax
import jax.numpy as jnp
import ml_dtypes
import numpy as np
from jax import lax
from jax.experimental import pallas as pl
from jax.experimental.pallas import tpu as pltpu
from jax.sharding import PartitionSpec as P

MESH = pl.DeviceIdType.MESH
NA, NR, AOI, AOI_START = 768, 12288, 256, 256
NP, NQ = 96, 128
NB = 256
ACQ, TILE = 8, 32
GROUPS = 3
CHUNKS = 3
FIRST = AOI_START // 3
KEPT = 88
PART = AOI // ACQ
DESTS = TILE


def split3(matrix):
    high = matrix.astype(ml_dtypes.bfloat16)
    low = (matrix - high.astype(np.float64)).astype(ml_dtypes.bfloat16)
    return np.concatenate([high, high, low], axis=1).astype(np.float32)


def dft_block(size):
    ids = np.arange(size)
    angle = 2.0 * np.pi * (np.outer(ids, ids) % size) / size
    c, s = np.cos(angle), np.sin(angle)
    return np.block([[c, s], [-s, c]])


def tables():
    left_p = split3(dft_block(NP))
    right_q = dft_block(NQ).T.astype(np.float32)
    left_b = dft_block(NB).astype(np.float32)
    angle = 2.0 * np.pi * np.outer(np.arange(NP), np.arange(NQ)) / NR
    twist = np.stack([np.cos(angle), -np.sin(angle)]).astype(np.float32)
    column = np.zeros((NB, 128), np.float64)
    ids = np.arange(NB)
    for a in (1, 2):
        column[:, 2 * a - 2] = np.cos(2.0 * np.pi * a * ids / NA)
        column[:, 2 * a - 1] = -np.sin(2.0 * np.pi * a * ids / NA)
    return left_p, right_q, left_b, twist, column.astype(np.float32)


def halves(value):
    high = value.astype(jnp.bfloat16)
    return high, (value - high.astype(jnp.float32)).astype(jnp.bfloat16)


def left_product(table, value):
    high, low = halves(value)
    rhs = jnp.concatenate([high, low, high], axis=0)
    return jnp.dot(table, rhs, preferred_element_type=jnp.float32)


def right_product(value, table):
    high, low = halves(value)
    lhs = jnp.concatenate([high, low, high], axis=1)
    return jnp.dot(lhs, table, preferred_element_type=jnp.float32)


def kernel(
    pairs, echo, filt, angle, left_p_h, right_q_h, left_b_h, twist_h, column_h,
    out_high, out_low,
    x, s, r, cs, ang, foc, gat0, gat1, gat2, sides, osend, orecv,
    fil_raw, fil_turn, fil, left_p_f, right_q_f, left_b_f, left_p, right_q, left_b, left_k, twist, column, pool, place, first_re, first_im,
    in_sem, turn_send, turn_recv, turn_own, acq_send, acq_recv, acq_own, out_send, out_recv, out_own,
):
    me_a, me_t = lax.axis_index("acq"), lax.axis_index("tile")
    gat = (gat0, gat1, gat2)
    outs = (out_high, out_low)

    def part_of(a):
        return 2 * lax.rem(me_t // 8 + a // 2, 4) + lax.rem(a, 2)

    me_part = part_of(me_a)

    early = [
        pltpu.make_async_copy(left_p_h, left_p_f, in_sem.at[0]),
        pltpu.make_async_copy(right_q_h, right_q_f, in_sem.at[1]),
        pltpu.make_async_copy(filt, fil_raw, in_sem.at[2]),
        pltpu.make_async_copy(twist_h, twist, in_sem.at[3]),
    ]
    lines = [pltpu.make_async_copy(echo.at[:, i], x.at[:, i], in_sem.at[4 + i]) for i in range(3)]
    late = [
        *[
            pltpu.make_async_copy(angle.at[:, pl.ds(128 * j, 128)], ang.at[j], in_sem.at[9 + j])
            for j in range(CHUNKS)
        ],
        pltpu.make_async_copy(left_b_h, left_b_f, in_sem.at[7]),
        pltpu.make_async_copy(column_h, column, in_sem.at[8]),
    ]
    for copy in early[:2] + lines[:2] + early[2:] + lines[2:] + late:
        copy.start()

    barrier = pltpu.get_barrier_semaphore()

    def greet_tile(k, _):
        peer = lax.rem(me_t + k, TILE)
        pl.semaphore_signal(barrier, inc=1, device_id={"tile": peer}, device_id_type=MESH)
        return 0

    def greet_acq(k, _):
        peer = lax.rem(me_a + k, ACQ)
        pl.semaphore_signal(barrier, inc=1, device_id={"acq": peer}, device_id_type=MESH)
        return 0

    lax.fori_loop(1, TILE, greet_tile, 0)
    lax.fori_loop(1, ACQ, greet_acq, 0)
    early[0].wait()
    left_p[...] = left_p_f[...].astype(jnp.bfloat16)
    early[1].wait()
    high, low = halves(right_q_f[...])
    right_q[...] = jnp.concatenate([high, high, low], axis=0)
    early[2].wait()
    lane = lax.broadcasted_iota(jnp.int32, (32, 128), 1)
    for c in range(2):
        v = [fil_raw[c, pl.ds(w, 32, stride=3), :] for w in range(3)]
        fil_turn[pl.ds(0, 32, stride=4), :] = v[0]
        fil_turn[pl.ds(1, 32, stride=4), :] = jnp.where(
            lane < 32, pltpu.roll(v[0], 32, 1), pltpu.roll(v[1], 32, 1)
        )
        fil_turn[pl.ds(2, 32, stride=4), :] = jnp.where(
            lane < 64, pltpu.roll(v[1], 64, 1), pltpu.roll(v[2], 64, 1)
        )
        fil_turn[pl.ds(3, 32, stride=4), :] = pltpu.roll(v[2], 96, 1)
        fil[c] = fil_turn[...].T[:NP]
    early[3].wait()
    lines[0].wait()
    lines[1].wait()

    def compress(g):
        for part in range(2):
            if g == 0 and part == 1:
                lines[2].wait()
            ids = range(4 * part, 4 * part + 4)
            value = jnp.concatenate(
                [
                    jnp.concatenate([x[c, (3 * i + g) // 8, pl.ds((3 * i + g) % 8, NP, stride=8), :] for i in ids], axis=1)
                    for c in range(2)
                ],
                axis=0,
            )
            value = left_product(left_p[...], value)
            tr, ti = twist[0], twist[1]
            rows = []
            for n in range(4):
                re = value[:NP, n * NQ : (n + 1) * NQ]
                im = value[NP:, n * NQ : (n + 1) * NQ]
                rows.append(jnp.concatenate([re * tr - im * ti, re * ti + im * tr], axis=1))
            value = right_product(jnp.concatenate(rows, axis=0), right_q[...])
            fr, fi = fil[0], fil[1]
            rows = []
            for n in range(4):
                re = value[n * NP : (n + 1) * NP, :NQ]
                im = value[n * NP : (n + 1) * NP, NQ:]
                rows.append(jnp.concatenate([re * fi + im * fr, re * fr - im * fi], axis=1))
            value = right_product(jnp.concatenate(rows, axis=0), right_q[...])
            top, low = [], []
            for n in range(4):
                im = value[n * NP : (n + 1) * NP, :NQ]
                re = value[n * NP : (n + 1) * NP, NQ:]
                top.append(im * tr - re * ti)
                low.append(re * tr + im * ti)
            value = jnp.concatenate(
                [jnp.concatenate(top, axis=1), jnp.concatenate(low, axis=1)], axis=0
            )
            value = left_product(left_p[...], value)
            for n, i in enumerate(ids):
                s[g, 1, pl.ds(i, NP, stride=8), :] = value[:NP, n * NQ : (n + 1) * NQ]
                s[g, 0, pl.ds(i, NP, stride=8), :] = value[NP:, n * NQ : (n + 1) * NQ]

    blocks = ((pl.ds(0, 1), pl.ds(0, 24)), (pl.ds(1, 2), pl.ds(0, 16)), (pl.ds(1, 2), pl.ds(16, 8)))

    def turn(block):
        groups, rows = blocks[block]

        def send(k, _):
            peer = lax.rem(me_t + k, TILE)
            pltpu.make_async_remote_copy(
                src_ref=s.at[groups, :, pl.ds(24 * peer + rows.start, rows.size), :],
                dst_ref=r.at[groups, :, me_t, rows, :],
                send_sem=turn_send.at[block],
                recv_sem=turn_recv.at[block],
                device_id={"tile": peer},
                device_id_type=MESH,
            ).start()
            return 0

        lax.fori_loop(1, TILE, send, 0)

    def turn_wait(block, sems):
        groups, rows = blocks[block]
        whole = r.at[groups, :, pl.ds(0, TILE - 1), rows, :]
        pltpu.make_async_copy(whole, whole, sems.at[block]).wait()

    compress(0)
    pl.semaphore_wait(barrier, (TILE - 1) + (ACQ - 1))
    turn(0)
    compress(1)
    compress(2)
    turn(1)
    turn(2)
    own_turn = pltpu.make_async_copy(
        s.at[:, :, pl.ds(24 * me_t, 24), :], r.at[:, :, me_t], turn_own
    )
    own_turn.start()
    for copy in late:
        copy.wait()
    high, low = halves(left_b_f[...])
    left_b[...] = jnp.concatenate([high, high, low], axis=1)
    kept = jnp.concatenate(
        [left_b_f[FIRST : FIRST + KEPT, :], left_b_f[NB + FIRST : NB + FIRST + KEPT, :]], axis=0
    )
    high, low = halves(kept)
    left_k[...] = jnp.concatenate([high, high, low], axis=1)
    row = lax.broadcasted_iota(jnp.int32, (1024, 128), 0)
    col = lax.broadcasted_iota(jnp.int32, (1024, 128), 1)
    same = jnp.logical_and(col // 16 == row // 128, col % 16 == row % 128 // 8)
    value = jnp.where(same, 1.0 / 16.0, 0.0).astype(jnp.bfloat16)
    pool[...] = jnp.concatenate([value, value], axis=0)
    same = jnp.logical_and(col // 16 == row // 128, col % 16 == row % 16)
    place[...] = jnp.where(same, 1.0, 0.0).astype(jnp.bfloat16)

    def phases(j):
        for h in range(12):
            rows = pl.ds(h * 64, 64)
            a = ang[j, rows, :]
            cs[j, 0, rows, :] = jnp.cos(a) * (1.0 / NA / NR)
            cs[j, 1, rows, :] = jnp.sin(a) * (1.0 / NA / NR)

    root = float(np.sqrt(0.75))

    def butterfly(re, im, sign):
        sr, si = re[1] + re[2], im[1] + im[2]
        dr, di = (re[1] - re[2]) * (sign * root), (im[1] - im[2]) * (sign * root)
        mr, mi = re[0] - 0.5 * sr, im[0] - 0.5 * si
        return [re[0] + sr, mr - di, mr + di], [im[0] + si, mi + dr, mi - dr]

    def transform(j, groups):
        value = jnp.concatenate(
            [
                jnp.concatenate(
                    [r[a, c, :, 8 * j : 8 * j + 8, :].reshape(NB, 128) for a in groups], axis=1
                )
                for c in range(2)
            ],
            axis=0,
        )
        value = left_product(left_b[...], value)
        parts = [slice(128 * n, 128 * n + 128) for n in range(len(groups))]
        return [value[:NB, n] for n in parts], [value[NB:, n] for n in parts]

    def focus(j):
        if j < CHUNKS - 1:
            re, im = transform(j, (0, 1, 2))
        else:
            re, im = transform(j, (1, 2))
            re, im = [first_re[...]] + re, [first_im[...]] + im
        for a in (1, 2):
            tr, ti = column[:, 2 * a - 2 : 2 * a - 1], column[:, 2 * a - 1 : 2 * a]
            re[a], im[a] = re[a] * tr - im[a] * ti, re[a] * ti + im[a] * tr
        re, im = butterfly(re, im, -1.0)
        for f1 in range(3):
            c, d = cs[j, 0, f1 * NB : (f1 + 1) * NB, :], cs[j, 1, f1 * NB : (f1 + 1) * NB, :]
            re[f1], im[f1] = re[f1] * c - im[f1] * d, re[f1] * d + im[f1] * c
        re, im = butterfly(re, im, 1.0)
        for a in (1, 2):
            tr, ti = column[:, 2 * a - 2 : 2 * a - 1], column[:, 2 * a - 1 : 2 * a]
            re[a], im[a] = re[a] * tr + im[a] * ti, im[a] * tr - re[a] * ti
        value = jnp.concatenate([jnp.concatenate(im, axis=1), jnp.concatenate(re, axis=1)], axis=0)
        value = left_product(left_k[...], value)
        for a in range(3):
            rows = pl.ds(8 + 3 * FIRST + a - AOI_START, 86, stride=3)
            foc[j, 1, rows, :] = value[:86, a * 128 : (a + 1) * 128]
            foc[j, 0, rows, :] = value[KEPT : KEPT + 86, a * 128 : (a + 1) * 128]

    def own_share(j):
        return pltpu.make_async_copy(
            foc.at[j, :, pl.ds(8 + me_part * PART, PART), :], gat[j].at[me_a], acq_own.at[j]
        )

    def share(j):
        def send(k, _):
            peer = lax.rem(me_a + k, ACQ)
            pltpu.make_async_remote_copy(
                src_ref=foc.at[j, :, pl.ds(8 + part_of(peer) * PART, PART), :],
                dst_ref=gat[j].at[me_a],
                send_sem=acq_send.at[j],
                recv_sem=acq_recv.at[j],
                device_id={"acq": peer},
                device_id_type=MESH,
            ).start()
            return 0

        lax.fori_loop(1, ACQ, send, 0)
        own_share(j).start()

    def take_share(j):
        whole = gat[j].at[pl.ds(0, ACQ - 1)]
        pltpu.make_async_copy(whole, whole, acq_recv.at[j]).wait()
        own_share(j).wait()

    def interfere(j):
        def line_up(a, _):
            rows = pl.ds(pl.multiple_of(a * PART, PART), PART)
            for c in range(2):
                sides[2, c, rows, :] = gat[j][a, c]
                for round_id in range(2):
                    sides[round_id, c, rows, :] = gat[j][pairs[round_id, a], c]
            return 0

        lax.fori_loop(0, ACQ, line_up, 0)
        re, im = [], []
        for round_id in range(2):
            for l in range(4):
                sum_re, sum_im = 0.0, 0.0
                for o in range(2):
                    rows = pl.ds(2 * l + o, DESTS, stride=8)
                    mr, mi = sides[2, 0, rows, :], sides[2, 1, rows, :]
                    pr, pi = sides[round_id, 0, rows, :], sides[round_id, 1, rows, :]
                    sum_re += mr * pr + mi * pi
                    sum_im += mi * pr - mr * pi
                re.append(sum_re)
                im.append(sum_im)
        value = jnp.concatenate([jnp.concatenate(re, axis=1), jnp.concatenate(im, axis=1)], axis=0)
        looked = jnp.dot(
            jnp.concatenate(halves(value), axis=1), pool[...], preferred_element_type=jnp.float32
        )
        for c in range(2):
            osend[j, c] = looked[c * DESTS : (c + 1) * DESTS].reshape(DESTS, 1, 128)

    has_own = me_t // 4 == me_part

    def send_out(j, first):
        def send(d, _):
            dest_a, dest_t = d // 4, 4 * me_part + lax.rem(d, 4)
            own = jnp.logical_and(dest_a == me_a, dest_t == me_t)

            @pl.when(jnp.logical_not(own))
            def _():
                pltpu.make_async_remote_copy(
                    src_ref=osend.at[pl.ds(first, j + 1 - first), :, d],
                    dst_ref=orecv.at[pl.ds(first, j + 1 - first), :, me_t],
                    send_sem=out_send.at[j],
                    recv_sem=out_recv.at[j],
                    device_id={"acq": dest_a, "tile": dest_t},
                    device_id_type=MESH,
                ).start()

            return 0

        lax.fori_loop(0, DESTS, send, 0)

        @pl.when(has_own)
        def _():
            own_out(j, first).start()

    def own_out(j, first):
        some = pl.ds(first, j + 1 - first)
        return pltpu.make_async_copy(
            osend.at[some, :, 4 * me_a + lax.rem(me_t, 4)], orecv.at[some, :, me_t], out_own.at[j]
        )

    def out_wait(j, first, sem):
        def wait(count):
            whole = orecv.at[pl.ds(first, j + 1 - first), :, pl.ds(0, count)]
            pltpu.make_async_copy(whole, whole, sem).wait()

        @pl.when(has_own)
        def _():
            wait(DESTS - 1)

        @pl.when(jnp.logical_not(has_own))
        def _():
            wait(DESTS)

    for j in range(CHUNKS):
        phases(j)
    own_turn.wait()
    turn_wait(0, turn_recv)
    (first_re[...],), (first_im[...],) = transform(CHUNKS - 1, (0,))
    turn_wait(1, turn_recv)
    for j in range(CHUNKS):
        if j == CHUNKS - 1:
            turn_wait(2, turn_recv)
        focus(j)
        share(j)
    for j in range(CHUNKS):
        take_share(j)
        interfere(j)
        if j == 1:
            send_out(1, 0)
        if j == 2:
            send_out(2, 2)
    for j in range(CHUNKS):
        turn_wait(j, turn_send)
        whole = gat[j].at[pl.ds(0, ACQ - 1)]
        pltpu.make_async_copy(whole, whole, acq_send.at[j]).wait()
    for j, first in ((1, 0), (2, 2)):
        out_wait(j, first, out_send.at[j])
        out_wait(j, first, out_recv.at[j])

        @pl.when(has_own)
        def _():
            own_out(j, first).wait()

    which = lax.broadcasted_iota(jnp.int32, (8, 128), 0)
    mask = lax.broadcasted_iota(jnp.int32, (8, 128), 1) // 16 == which
    spreads = []
    for c in range(2):
        for v in range(12):
            pieces = [(u // CHUNKS, u % CHUNKS) for u in range(8 * v, 8 * v + 8)]
            spread = [jnp.where(mask, orecv[j, c, t], 0.0) for t, j in pieces]
            spreads.append(jnp.concatenate(spread, axis=1))
    value = jnp.concatenate(spreads, axis=0)
    for n, part in enumerate(halves(value)):
        value = jnp.dot(part, place[...], preferred_element_type=jnp.float32)
        for c in range(2):
            for v in range(12):
                for round_id in range(2):
                    first = (c * 12 + v) * 8 + 4 * round_id
                    outs[n][c, round_id, v] = value[first : first + 4]


def shards(unprocessed_echo_data, slant_kernel_frequencies, along_track_kernel_angle, pairs):
    echo = unprocessed_echo_data.reshape(2, GROUPS, 8, NP, NQ)
    echo = echo.transpose(0, 1, 3, 2, 4).reshape(2, GROUPS, NP * 8, NQ)
    filt = slant_kernel_frequencies.reshape(2, NP, NQ)
    angle = along_track_kernel_angle[0]
    consts = [jnp.asarray(t) for t in tables()]
    any_spec = pl.BlockSpec(memory_space=pl.ANY)
    f32 = jnp.float32
    vmem, dma = pltpu.VMEM, pltpu.SemaphoreType.DMA
    high, low = pl.pallas_call(
        kernel,
        out_shape=[jax.ShapeDtypeStruct((2, 2, 12, 4, 128), f32)] * 2,
        in_specs=[pl.BlockSpec(memory_space=pltpu.SMEM)] + [any_spec] * 8,
        out_specs=[pl.BlockSpec(memory_space=pltpu.VMEM)] * 2,
        scratch_shapes=[
            vmem((2, GROUPS, NP * 8, NQ), f32),
            vmem((GROUPS, 2, NP * 8, NQ), f32),
            vmem((GROUPS, 2, TILE, 8 * CHUNKS, 128), f32),
            vmem((CHUNKS, 2, NA, 128), f32),
            vmem((CHUNKS, NA, 128), f32),
            vmem((CHUNKS, 2, AOI + 16, 128), f32),
            vmem((ACQ, 2, PART, 128), f32),
            vmem((ACQ, 2, PART, 128), f32),
            vmem((ACQ, 2, PART, 128), f32),
            vmem((3, 2, ACQ * PART, 128), f32),
            vmem((CHUNKS, 2, DESTS, 1, 128), f32),
            vmem((CHUNKS, 2, DESTS, 1, 128), f32),
            vmem((2, NP, NQ), f32),
            vmem((NQ, 128), f32),
            vmem((2, NP, NQ), f32),
            vmem((2 * NP, 6 * NP), f32),
            vmem((2 * NQ, 2 * NQ), f32),
            vmem((2 * NB, 2 * NB), f32),
            vmem((2 * NP, 6 * NP), jnp.bfloat16),
            vmem((6 * NQ, 2 * NQ), jnp.bfloat16),
            vmem((2 * NB, 6 * NB), jnp.bfloat16),
            vmem((2 * KEPT, 6 * NB), jnp.bfloat16),
            vmem((2, NP, NQ), f32),
            vmem((NB, 128), f32),
            vmem((2 * 8 * 128, 128), jnp.bfloat16),
            vmem((8 * 128, 128), jnp.bfloat16),
            vmem((NB, 128), f32),
            vmem((NB, 128), f32),
            dma((12,)),
            dma((CHUNKS,)),
            dma((CHUNKS,)),
            dma,
            dma((CHUNKS,)),
            dma((CHUNKS,)),
            dma((CHUNKS,)),
            dma((CHUNKS,)),
            dma((CHUNKS,)),
            dma((CHUNKS,)),
        ],
        name="range_doppler",
        compiler_params=pltpu.CompilerParams(
            collective_id=0, has_side_effects=True, vmem_limit_bytes=56 * 2**20
        ),
    )(pairs, echo, filt, angle, *consts)

    def lay_out(value):
        return value.transpose(0, 1, 3, 2, 4).reshape(2, 2, 1, 4, NR // 8)

    return lay_out(high) + lay_out(low)


def solution(mesh):
    in_specs = (P(None, "acq", "tile", None), P(None, "acq", None), P("acq", None, "tile"), P())
    out_specs = P(None, None, "acq", "tile", None)
    return jax.shard_map(shards, mesh=mesh, in_specs=in_specs, out_specs=out_specs, check_vma=False)
```

```python
import jax
import jax.numpy as jnp
import ml_dtypes
import numpy as np
from jax import lax
from jax.experimental import pallas as pl
from jax.experimental.layout import Layout, with_layout_constraint
from jax.experimental.pallas import tpu as pltpu
from jax.sharding import PartitionSpec as P

MESH = pl.DeviceIdType.MESH
NA, NR, AOI, AOI_START = 768, 12288, 256, 256
NP, NQ = 96, 128
NB = 256
ACQ, TILE = 8, 32
GROUPS = 3
CHUNKS = 3
FIRST = AOI_START // 3
KEPT = 88
PART = AOI // ACQ
DESTS = TILE


def split3(matrix):
    high = matrix.astype(ml_dtypes.bfloat16)
    low = (matrix - high.astype(np.float64)).astype(ml_dtypes.bfloat16)
    return np.concatenate([high, high, low], axis=1).astype(np.float32)


def dft_block(size):
    ids = np.arange(size)
    angle = 2.0 * np.pi * (np.outer(ids, ids) % size) / size
    c, s = np.cos(angle), np.sin(angle)
    return np.block([[c, s], [-s, c]])


def tables():
    left_p = split3(dft_block(NP))
    right_q = dft_block(NQ).T.astype(np.float32)
    left_b = dft_block(NB).astype(np.float32)
    angle = 2.0 * np.pi * np.outer(np.arange(NP), np.arange(NQ)) / NR
    twist = np.stack([np.cos(angle), -np.sin(angle)]).astype(np.float32)
    column = np.zeros((NB, 128), np.float64)
    ids = np.arange(NB)
    for a in (1, 2):
        column[:, 2 * a - 2] = np.cos(2.0 * np.pi * a * ids / NA)
        column[:, 2 * a - 1] = -np.sin(2.0 * np.pi * a * ids / NA)
    return left_p, right_q, left_b, twist, column.astype(np.float32)


def halves(value):
    high = value.astype(jnp.bfloat16)
    return high, (value - high.astype(jnp.float32)).astype(jnp.bfloat16)


def left_product(table, value):
    high, low = halves(value)
    rhs = jnp.concatenate([high, low, high], axis=0)
    return jnp.dot(table, rhs, preferred_element_type=jnp.float32)


def right_product(value, table):
    high, low = halves(value)
    lhs = jnp.concatenate([high, low, high], axis=1)
    return jnp.dot(lhs, table, preferred_element_type=jnp.float32)


def kernel(
    pairs, echo, filt, angle, left_p_h, right_q_h, left_b_h, twist_h, column_h,
    out_high, out_low,
    x, s, r, cs, ang, foc, gat0, gat1, gat2, sides, osend, orecv,
    fil_raw, fil_turn, fil, left_p_f, right_q_f, left_b_f, left_p, right_q, left_b, left_k, twist, column, wide, pool, place, first_re, first_im,
    in_sem, turn_send, turn_recv, turn_own, acq_send, acq_recv, acq_own, out_send, out_recv, out_own,
):
    me_a, me_t = lax.axis_index("acq"), lax.axis_index("tile")
    gat = (gat0, gat1, gat2)
    outs = (out_high, out_low)

    def part_of(a):
        return 2 * lax.rem(me_t // 8 + a // 2, 4) + lax.rem(a, 2)

    me_part = part_of(me_a)

    def far_first(k):
        return 4 + (k + 1) // 2 * (2 * lax.rem(k, 2) - 1)


    early = [
        pltpu.make_async_copy(left_p_h, left_p_f, in_sem.at[0]),
        pltpu.make_async_copy(right_q_h, right_q_f, in_sem.at[1]),
        pltpu.make_async_copy(filt, fil_raw, in_sem.at[2]),
        pltpu.make_async_copy(twist_h, twist, in_sem.at[3]),
    ]
    lines = [pltpu.make_async_copy(echo.at[:, i], x.at[:, i], in_sem.at[4 + i]) for i in range(3)]
    late = [
        *[
            pltpu.make_async_copy(angle.at[:, pl.ds(128 * j, 128)], ang.at[j], in_sem.at[9 + j])
            for j in range(CHUNKS)
        ],
        pltpu.make_async_copy(left_b_h, left_b_f, in_sem.at[7]),
        pltpu.make_async_copy(column_h, column, in_sem.at[8]),
    ]
    for copy in early[:2] + lines[:2] + early[2:] + lines[2:] + late:
        copy.start()

    barrier = pltpu.get_barrier_semaphore()

    def greet_tile(k, _):
        peer = lax.rem(me_t + k, TILE)
        pl.semaphore_signal(barrier, inc=1, device_id={"tile": peer}, device_id_type=MESH)
        return 0

    def greet_acq(k, _):
        peer = lax.rem(me_a + k, ACQ)
        pl.semaphore_signal(barrier, inc=1, device_id={"acq": peer}, device_id_type=MESH)
        return 0

    lax.fori_loop(1, TILE, greet_tile, 0)
    lax.fori_loop(1, ACQ, greet_acq, 0)
    early[0].wait()
    left_p[...] = left_p_f[...].astype(jnp.bfloat16)
    early[1].wait()
    high, low = halves(right_q_f[...])
    right_q[...] = jnp.concatenate([high, high, low], axis=0)
    early[2].wait()
    lane = lax.broadcasted_iota(jnp.int32, (32, 128), 1)
    for c in range(2):
        v = [fil_raw[c, pl.ds(w, 32, stride=3), :] for w in range(3)]
        fil_turn[pl.ds(0, 32, stride=4), :] = v[0]
        fil_turn[pl.ds(1, 32, stride=4), :] = jnp.where(
            lane < 32, pltpu.roll(v[0], 32, 1), pltpu.roll(v[1], 32, 1)
        )
        fil_turn[pl.ds(2, 32, stride=4), :] = jnp.where(
            lane < 64, pltpu.roll(v[1], 64, 1), pltpu.roll(v[2], 64, 1)
        )
        fil_turn[pl.ds(3, 32, stride=4), :] = pltpu.roll(v[2], 96, 1)
        fil[c] = fil_turn[...].T[:NP]
    early[3].wait()
    lines[0].wait()
    lines[1].wait()

    def compress(g):
        for part in range(2):
            if g == 0 and part == 1:
                lines[2].wait()
            ids = range(4 * part, 4 * part + 4)
            value = jnp.concatenate(
                [
                    jnp.concatenate([x[c, (3 * i + g) // 8, pl.ds((3 * i + g) % 8, NP, stride=8), :] for i in ids], axis=1)
                    for c in range(2)
                ],
                axis=0,
            )
            value = left_product(left_p[...], value)
            tr, ti = twist[0], twist[1]
            rows = []
            for n in range(4):
                re = value[:NP, n * NQ : (n + 1) * NQ]
                im = value[NP:, n * NQ : (n + 1) * NQ]
                rows.append(jnp.concatenate([re * tr - im * ti, re * ti + im * tr], axis=1))
            value = right_product(jnp.concatenate(rows, axis=0), right_q[...])
            fr, fi = fil[0], fil[1]
            rows = []
            for n in range(4):
                re = value[n * NP : (n + 1) * NP, :NQ]
                im = value[n * NP : (n + 1) * NP, NQ:]
                rows.append(jnp.concatenate([re * fi + im * fr, re * fr - im * fi], axis=1))
            value = right_product(jnp.concatenate(rows, axis=0), right_q[...])
            top, low = [], []
            for n in range(4):
                im = value[n * NP : (n + 1) * NP, :NQ]
                re = value[n * NP : (n + 1) * NP, NQ:]
                top.append(im * tr - re * ti)
                low.append(re * tr + im * ti)
            value = jnp.concatenate(
                [jnp.concatenate(top, axis=1), jnp.concatenate(low, axis=1)], axis=0
            )
            value = left_product(left_p[...], value)
            for n, i in enumerate(ids):
                s[g, 1, pl.ds(i, NP, stride=8), :] = value[:NP, n * NQ : (n + 1) * NQ]
                s[g, 0, pl.ds(i, NP, stride=8), :] = value[NP:, n * NQ : (n + 1) * NQ]

    blocks = ((pl.ds(0, 1), pl.ds(0, 24)), (pl.ds(1, 2), pl.ds(0, 16)), (pl.ds(1, 2), pl.ds(16, 8)))

    def turn(block):
        groups, rows = blocks[block]

        def send(k, _):
            peer = lax.rem(me_t + k, TILE)
            pltpu.make_async_remote_copy(
                src_ref=s.at[groups, :, pl.ds(24 * peer + rows.start, rows.size), :],
                dst_ref=r.at[groups, :, me_t, rows, :],
                send_sem=turn_send.at[block],
                recv_sem=turn_recv.at[block],
                device_id={"tile": peer},
                device_id_type=MESH,
            ).start()
            return 0

        lax.fori_loop(1, TILE, send, 0)

    def turn_wait(block, sems):
        groups, rows = blocks[block]
        whole = r.at[groups, :, pl.ds(0, TILE - 1), rows, :]
        pltpu.make_async_copy(whole, whole, sems.at[block]).wait()

    compress(0)
    pl.semaphore_wait(barrier, (TILE - 1) + (ACQ - 1))
    turn(0)
    compress(1)
    compress(2)
    turn(1)
    turn(2)
    own_turn = pltpu.make_async_copy(
        s.at[:, :, pl.ds(24 * me_t, 24), :], r.at[:, :, me_t], turn_own
    )
    own_turn.start()
    for copy in late:
        copy.wait()
    for n in range(4):
        wide[n] = jnp.broadcast_to(column[:, n : n + 1], (NB, 128))
    high, low = halves(left_b_f[...])
    left_b[...] = jnp.concatenate([high, high, low], axis=1)
    kept = jnp.concatenate(
        [left_b_f[FIRST : FIRST + KEPT, :], left_b_f[NB + FIRST : NB + FIRST + KEPT, :]], axis=0
    )
    high, low = halves(kept)
    left_k[...] = jnp.concatenate([high, high, low], axis=1)
    row = lax.broadcasted_iota(jnp.int32, (1024, 128), 0)
    col = lax.broadcasted_iota(jnp.int32, (1024, 128), 1)
    same = jnp.logical_and(col // 16 == row // 128, col % 16 == row % 128 // 8)
    value = jnp.where(same, 1.0 / 16.0, 0.0).astype(jnp.bfloat16)
    pool[...] = jnp.concatenate([value, value], axis=0)
    same = jnp.logical_and(col // 16 == row // 128, col % 16 == row % 16)
    place[...] = jnp.where(same, 1.0, 0.0).astype(jnp.bfloat16)

    def phases(j):
        for h in range(12):
            rows = pl.ds(h * 64, 64)
            a = ang[j, rows, :]
            cs[j, 0, rows, :] = jnp.cos(a) * (1.0 / NA / NR)
            cs[j, 1, rows, :] = jnp.sin(a) * (1.0 / NA / NR)

    root = float(np.sqrt(0.75))

    def butterfly(re, im, sign):
        sr, si = re[1] + re[2], im[1] + im[2]
        dr, di = (re[1] - re[2]) * (sign * root), (im[1] - im[2]) * (sign * root)
        mr, mi = re[0] - 0.5 * sr, im[0] - 0.5 * si
        return [re[0] + sr, mr - di, mr + di], [im[0] + si, mi + dr, mi - dr]

    def transform(j, groups):
        value = jnp.concatenate(
            [
                jnp.concatenate(
                    [r[a, c, :, 8 * j : 8 * j + 8, :].reshape(NB, 128) for a in groups], axis=1
                )
                for c in range(2)
            ],
            axis=0,
        )
        value = left_product(left_b[...], value)
        parts = [slice(128 * n, 128 * n + 128) for n in range(len(groups))]
        return [value[:NB, n] for n in parts], [value[NB:, n] for n in parts]

    def focus(j):
        if j < CHUNKS - 1:
            re, im = transform(j, (0, 1, 2))
        else:
            re, im = transform(j, (1, 2))
            re, im = [first_re[...]] + re, [first_im[...]] + im
        for a in (1, 2):
            tr, ti = wide[2 * a - 2], wide[2 * a - 1]
            re[a], im[a] = re[a] * tr - im[a] * ti, re[a] * ti + im[a] * tr
        re, im = butterfly(re, im, -1.0)
        for f1 in range(3):
            c, d = cs[j, 0, f1 * NB : (f1 + 1) * NB, :], cs[j, 1, f1 * NB : (f1 + 1) * NB, :]
            re[f1], im[f1] = re[f1] * c - im[f1] * d, re[f1] * d + im[f1] * c
        re, im = butterfly(re, im, 1.0)
        for a in (1, 2):
            tr, ti = wide[2 * a - 2], wide[2 * a - 1]
            re[a], im[a] = re[a] * tr + im[a] * ti, im[a] * tr - re[a] * ti
        value = jnp.concatenate([jnp.concatenate(im, axis=1), jnp.concatenate(re, axis=1)], axis=0)
        value = left_product(left_k[...], value)
        for a in range(3):
            rows = pl.ds(8 + 3 * FIRST + a - AOI_START, 86, stride=3)
            foc[j, 1, rows, :] = value[:86, a * 128 : (a + 1) * 128]
            foc[j, 0, rows, :] = value[KEPT : KEPT + 86, a * 128 : (a + 1) * 128]

    def own_share(j):
        return pltpu.make_async_copy(
            foc.at[j, :, pl.ds(8 + me_part * PART, PART), :], gat[j].at[me_a], acq_own.at[j]
        )

    def share(j):
        def send(k, _):
            peer = lax.rem(me_a + far_first(k), ACQ)
            pltpu.make_async_remote_copy(
                src_ref=foc.at[j, :, pl.ds(8 + part_of(peer) * PART, PART), :],
                dst_ref=gat[j].at[me_a],
                send_sem=acq_send.at[j],
                recv_sem=acq_recv.at[j],
                device_id={"acq": peer},
                device_id_type=MESH,
            ).start()
            return 0

        lax.fori_loop(0, ACQ - 1, send, 0)
        own_share(j).start()

    def take_share(j):
        whole = gat[j].at[pl.ds(0, ACQ - 1)]
        pltpu.make_async_copy(whole, whole, acq_recv.at[j]).wait()
        own_share(j).wait()

    def interfere(j):
        def line_up(a, _):
            rows = pl.ds(pl.multiple_of(a * PART, PART), PART)
            for c in range(2):
                sides[2, c, rows, :] = gat[j][a, c]
                for round_id in range(2):
                    sides[round_id, c, rows, :] = gat[j][pairs[round_id, a], c]
            return 0

        lax.fori_loop(0, ACQ, line_up, 0)
        re, im = [], []
        for round_id in range(2):
            for l in range(4):
                sum_re, sum_im = 0.0, 0.0
                for o in range(2):
                    rows = pl.ds(2 * l + o, DESTS, stride=8)
                    mr, mi = sides[2, 0, rows, :], sides[2, 1, rows, :]
                    pr, pi = sides[round_id, 0, rows, :], sides[round_id, 1, rows, :]
                    sum_re += mr * pr + mi * pi
                    sum_im += mi * pr - mr * pi
                re.append(sum_re)
                im.append(sum_im)
        value = jnp.concatenate([jnp.concatenate(re, axis=1), jnp.concatenate(im, axis=1)], axis=0)
        looked = jnp.dot(
            jnp.concatenate(halves(value), axis=1), pool[...], preferred_element_type=jnp.float32
        )
        for c in range(2):
            osend[j, c] = looked[c * DESTS : (c + 1) * DESTS].reshape(DESTS, 1, 128)

    has_own = me_t // 4 == me_part

    def send_out(j, first):
        def send(d, _):
            dest_a = lax.rem(me_a + far_first(d // 4), ACQ)
            dest_t = 4 * me_part + lax.rem(d, 4)
            own = jnp.logical_and(dest_a == me_a, dest_t == me_t)

            @pl.when(jnp.logical_not(own))
            def _():
                pltpu.make_async_remote_copy(
                    src_ref=osend.at[pl.ds(first, j + 1 - first), :, 4 * dest_a + lax.rem(d, 4)],
                    dst_ref=orecv.at[pl.ds(first, j + 1 - first), :, me_t],
                    send_sem=out_send.at[j],
                    recv_sem=out_recv.at[j],
                    device_id={"acq": dest_a, "tile": dest_t},
                    device_id_type=MESH,
                ).start()

            return 0

        lax.fori_loop(0, DESTS, send, 0)

        @pl.when(has_own)
        def _():
            own_out(j, first).start()

    def own_out(j, first):
        some = pl.ds(first, j + 1 - first)
        return pltpu.make_async_copy(
            osend.at[some, :, 4 * me_a + lax.rem(me_t, 4)], orecv.at[some, :, me_t], out_own.at[j]
        )

    def out_wait(j, first, sem):
        def wait(count):
            whole = orecv.at[pl.ds(first, j + 1 - first), :, pl.ds(0, count)]
            pltpu.make_async_copy(whole, whole, sem).wait()

        @pl.when(has_own)
        def _():
            wait(DESTS - 1)

        @pl.when(jnp.logical_not(has_own))
        def _():
            wait(DESTS)

    for j in range(CHUNKS):
        phases(j)
    own_turn.wait()
    turn_wait(0, turn_recv)
    (first_re[...],), (first_im[...],) = transform(CHUNKS - 1, (0,))
    turn_wait(1, turn_recv)
    for j in range(CHUNKS):
        if j == CHUNKS - 1:
            turn_wait(2, turn_recv)
        focus(j)
        share(j)
    for j in range(CHUNKS):
        take_share(j)
        interfere(j)
        if j == 1:
            send_out(1, 0)
        if j == 2:
            send_out(2, 2)
    for j in range(CHUNKS):
        turn_wait(j, turn_send)
        whole = gat[j].at[pl.ds(0, ACQ - 1)]
        pltpu.make_async_copy(whole, whole, acq_send.at[j]).wait()
    for j, first in ((1, 0), (2, 2)):
        out_wait(j, first, out_send.at[j])
        out_wait(j, first, out_recv.at[j])

        @pl.when(has_own)
        def _():
            own_out(j, first).wait()

    which = lax.broadcasted_iota(jnp.int32, (8, 128), 0)
    mask = lax.broadcasted_iota(jnp.int32, (8, 128), 1) // 16 == which
    spreads = []
    for c in range(2):
        for v in range(12):
            pieces = [(u // CHUNKS, u % CHUNKS) for u in range(8 * v, 8 * v + 8)]
            spread = [jnp.where(mask, orecv[j, c, t], 0.0) for t, j in pieces]
            spreads.append(jnp.concatenate(spread, axis=1))
    value = jnp.concatenate(spreads, axis=0)
    for out, part in zip(outs, halves(value)):
        value = jnp.dot(part, place[...], preferred_element_type=jnp.float32)
        for c in range(2):
            for v in range(12):
                for round_id in range(2):
                    first = (c * 12 + v) * 8 + 4 * round_id
                    rows = (c * 2 + round_id) * 48 + 4 * v
                    out[rows : rows + 4, :] = value[first : first + 4]


def shards(unprocessed_echo_data, slant_kernel_frequencies, along_track_kernel_angle, pairs):
    echo = unprocessed_echo_data.reshape(2, GROUPS, 8, NP, NQ)
    echo = echo.transpose(0, 1, 3, 2, 4).reshape(2, GROUPS, NP * 8, NQ)
    filt = slant_kernel_frequencies.reshape(2, NP, NQ)
    angle = along_track_kernel_angle[0]
    consts = [jnp.asarray(t) for t in tables()]
    any_spec = pl.BlockSpec(memory_space=pl.ANY)
    f32 = jnp.float32
    vmem, dma = pltpu.VMEM, pltpu.SemaphoreType.DMA
    high, low = pl.pallas_call(
        kernel,
        out_shape=[vmem((2 * 2 * 12 * 4, 128), f32)] * 2,
        in_specs=[pl.BlockSpec(memory_space=pltpu.SMEM)] + [any_spec] * 8,
        out_specs=[pl.BlockSpec(memory_space=pltpu.VMEM)] * 2,
        scratch_shapes=[
            vmem((2, GROUPS, NP * 8, NQ), f32),
            vmem((GROUPS, 2, NP * 8, NQ), f32),
            vmem((GROUPS, 2, TILE, 8 * CHUNKS, 128), f32),
            vmem((CHUNKS, 2, NA, 128), f32),
            vmem((CHUNKS, NA, 128), f32),
            vmem((CHUNKS, 2, AOI + 16, 128), f32),
            vmem((ACQ, 2, PART, 128), f32),
            vmem((ACQ, 2, PART, 128), f32),
            vmem((ACQ, 2, PART, 128), f32),
            vmem((3, 2, ACQ * PART, 128), f32),
            vmem((CHUNKS, 2, DESTS, 1, 128), f32),
            vmem((CHUNKS, 2, DESTS, 1, 128), f32),
            vmem((2, NP, NQ), f32),
            vmem((NQ, 128), f32),
            vmem((2, NP, NQ), f32),
            vmem((2 * NP, 6 * NP), f32),
            vmem((2 * NQ, 2 * NQ), f32),
            vmem((2 * NB, 2 * NB), f32),
            vmem((2 * NP, 6 * NP), jnp.bfloat16),
            vmem((6 * NQ, 2 * NQ), jnp.bfloat16),
            vmem((2 * NB, 6 * NB), jnp.bfloat16),
            vmem((2 * KEPT, 6 * NB), jnp.bfloat16),
            vmem((2, NP, NQ), f32),
            vmem((NB, 128), f32),
            vmem((4, NB, 128), f32),
            vmem((2 * 8 * 128, 128), jnp.bfloat16),
            vmem((8 * 128, 128), jnp.bfloat16),
            vmem((NB, 128), f32),
            vmem((NB, 128), f32),
            dma((12,)),
            dma((CHUNKS,)),
            dma((CHUNKS,)),
            dma,
            dma((CHUNKS,)),
            dma((CHUNKS,)),
            dma((CHUNKS,)),
            dma((CHUNKS,)),
            dma((CHUNKS,)),
            dma((CHUNKS,)),
        ],
        name="range_doppler",
        compiler_params=pltpu.CompilerParams(
            collective_id=0, has_side_effects=True, vmem_limit_bytes=56 * 2**20
        ),
    )(pairs, echo, filt, angle, *consts)

    rows = (high + low).reshape(2, 2, 12, 4, 128).transpose(0, 1, 3, 2, 4)
    rows = with_layout_constraint(rows, Layout((0, 1, 3, 2, 4)))
    return rows.reshape(2, 2, 1, 4, NR // 8)


def solution(mesh):
    in_specs = (P(None, "acq", "tile", None), P(None, "acq", None), P("acq", None, "tile"), P())
    out_specs = P(None, None, "acq", "tile", None)
    return jax.shard_map(shards, mesh=mesh, in_specs=in_specs, out_specs=out_specs, check_vma=False)
```

```python
import jax
import jax.numpy as jnp
import ml_dtypes
import numpy as np
from jax import lax
from jax.experimental import pallas as pl
from jax.experimental.layout import Layout, with_layout_constraint
from jax.experimental.pallas import tpu as pltpu
from jax.sharding import PartitionSpec as P

MESH = pl.DeviceIdType.MESH
NA, NR, AOI, AOI_START = 768, 12288, 256, 256
NP, NQ = 96, 128
NB = 256
ACQ, TILE = 8, 32
GROUPS = 3
CHUNKS = 3
FIRST = AOI_START // 3
KEPT = 88
PART = AOI // ACQ
DESTS = TILE


def split3(matrix):
    high = matrix.astype(ml_dtypes.bfloat16)
    low = (matrix - high.astype(np.float64)).astype(ml_dtypes.bfloat16)
    return np.concatenate([high, high, low], axis=1).astype(np.float32)


def dft_block(size):
    ids = np.arange(size)
    angle = 2.0 * np.pi * (np.outer(ids, ids) % size) / size
    c, s = np.cos(angle), np.sin(angle)
    return np.block([[c, s], [-s, c]])


def tables():
    left_p = split3(dft_block(NP))
    right_q = dft_block(NQ).T.astype(np.float32)
    left_b = dft_block(NB).astype(np.float32)
    angle = 2.0 * np.pi * np.outer(np.arange(NP), np.arange(NQ)) / NR
    twist = np.stack([np.cos(angle), -np.sin(angle)]).astype(np.float32)
    column = np.zeros((NB, 128), np.float64)
    ids = np.arange(NB)
    for a in (1, 2):
        column[:, 2 * a - 2] = np.cos(2.0 * np.pi * a * ids / NA)
        column[:, 2 * a - 1] = -np.sin(2.0 * np.pi * a * ids / NA)
    return left_p, right_q, left_b, twist, column.astype(np.float32)


def halves(value):
    high = value.astype(jnp.bfloat16)
    return high, (value - high.astype(jnp.float32)).astype(jnp.bfloat16)


def left_product(table, value):
    high, low = halves(value)
    rhs = jnp.concatenate([high, low, high], axis=0)
    return jnp.dot(table, rhs, preferred_element_type=jnp.float32)


def right_product(value, table):
    high, low = halves(value)
    lhs = jnp.concatenate([high, low, high], axis=1)
    return jnp.dot(lhs, table, preferred_element_type=jnp.float32)


def kernel(
    pairs, echo, filt, angle, left_p_h, right_q_h, left_b_h, twist_h, column_h,
    out_early, out_late,
    x, s, r, cs, ang, foc, gat0, gat1, gat2, sides, osend, orecv,
    fil_raw, fil_turn, fil, left_p_f, right_q_f, left_b_f, left_p, right_q, left_b, left_k, twist, column, wide, pool, place, first_re, first_im,
    in_sem, turn_send, turn_recv, turn_own, acq_send, acq_recv, acq_own, out_send, out_recv, out_own,
):
    me_a, me_t = lax.axis_index("acq"), lax.axis_index("tile")
    gat = (gat0, gat1, gat2)

    def part_of(a):
        return 2 * lax.rem(me_t // 8 + a // 2, 4) + lax.rem(a, 2)

    me_part = part_of(me_a)

    def far_first(k):
        return 4 + (k + 1) // 2 * (2 * lax.rem(k, 2) - 1)


    early = [
        pltpu.make_async_copy(left_p_h, left_p_f, in_sem.at[0]),
        pltpu.make_async_copy(right_q_h, right_q_f, in_sem.at[1]),
        pltpu.make_async_copy(filt, fil_raw, in_sem.at[2]),
        pltpu.make_async_copy(twist_h, twist, in_sem.at[3]),
    ]
    lines = [pltpu.make_async_copy(echo.at[:, i], x.at[:, i], in_sem.at[4 + i]) for i in range(3)]
    late = [
        *[
            pltpu.make_async_copy(angle.at[:, pl.ds(128 * j, 128)], ang.at[j], in_sem.at[9 + j])
            for j in range(CHUNKS)
        ],
        pltpu.make_async_copy(left_b_h, left_b_f, in_sem.at[7]),
        pltpu.make_async_copy(column_h, column, in_sem.at[8]),
    ]
    for copy in early[:2] + lines[:2] + early[2:] + lines[2:] + late:
        copy.start()

    barrier = pltpu.get_barrier_semaphore()

    def greet_tile(k, _):
        peer = lax.rem(me_t + k, TILE)
        pl.semaphore_signal(barrier, inc=1, device_id={"tile": peer}, device_id_type=MESH)
        return 0

    def greet_acq(k, _):
        peer = lax.rem(me_a + k, ACQ)
        pl.semaphore_signal(barrier, inc=1, device_id={"acq": peer}, device_id_type=MESH)
        return 0

    lax.fori_loop(1, TILE, greet_tile, 0)
    lax.fori_loop(1, ACQ, greet_acq, 0)
    early[0].wait()
    left_p[...] = left_p_f[...].astype(jnp.bfloat16)
    early[1].wait()
    high, low = halves(right_q_f[...])
    right_q[...] = jnp.concatenate([high, high, low], axis=0)
    early[2].wait()
    lane = lax.broadcasted_iota(jnp.int32, (32, 128), 1)
    for c in range(2):
        v = [fil_raw[c, pl.ds(w, 32, stride=3), :] for w in range(3)]
        fil_turn[pl.ds(0, 32, stride=4), :] = v[0]
        fil_turn[pl.ds(1, 32, stride=4), :] = jnp.where(
            lane < 32, pltpu.roll(v[0], 32, 1), pltpu.roll(v[1], 32, 1)
        )
        fil_turn[pl.ds(2, 32, stride=4), :] = jnp.where(
            lane < 64, pltpu.roll(v[1], 64, 1), pltpu.roll(v[2], 64, 1)
        )
        fil_turn[pl.ds(3, 32, stride=4), :] = pltpu.roll(v[2], 96, 1)
        fil[c] = fil_turn[...].T[:NP]
    early[3].wait()
    lines[0].wait()
    lines[1].wait()

    def compress(g):
        for part in range(2):
            if g == 0 and part == 1:
                lines[2].wait()
            ids = range(4 * part, 4 * part + 4)
            value = jnp.concatenate(
                [
                    jnp.concatenate([x[c, (3 * i + g) // 8, pl.ds((3 * i + g) % 8, NP, stride=8), :] for i in ids], axis=1)
                    for c in range(2)
                ],
                axis=0,
            )
            value = left_product(left_p[...], value)
            tr, ti = twist[0], twist[1]
            rows = []
            for n in range(4):
                re = value[:NP, n * NQ : (n + 1) * NQ]
                im = value[NP:, n * NQ : (n + 1) * NQ]
                rows.append(jnp.concatenate([re * tr - im * ti, re * ti + im * tr], axis=1))
            value = right_product(jnp.concatenate(rows, axis=0), right_q[...])
            fr, fi = fil[0], fil[1]
            rows = []
            for n in range(4):
                re = value[n * NP : (n + 1) * NP, :NQ]
                im = value[n * NP : (n + 1) * NP, NQ:]
                rows.append(jnp.concatenate([re * fi + im * fr, re * fr - im * fi], axis=1))
            value = right_product(jnp.concatenate(rows, axis=0), right_q[...])
            top, low = [], []
            for n in range(4):
                im = value[n * NP : (n + 1) * NP, :NQ]
                re = value[n * NP : (n + 1) * NP, NQ:]
                top.append(im * tr - re * ti)
                low.append(re * tr + im * ti)
            value = jnp.concatenate(
                [jnp.concatenate(top, axis=1), jnp.concatenate(low, axis=1)], axis=0
            )
            value = left_product(left_p[...], value)
            for n, i in enumerate(ids):
                s[g, 1, pl.ds(i, NP, stride=8), :] = value[:NP, n * NQ : (n + 1) * NQ]
                s[g, 0, pl.ds(i, NP, stride=8), :] = value[NP:, n * NQ : (n + 1) * NQ]

    blocks = ((pl.ds(0, 1), pl.ds(0, 24)), (pl.ds(1, 2), pl.ds(0, 16)), (pl.ds(1, 2), pl.ds(16, 8)))

    def turn(block):
        groups, rows = blocks[block]

        def send(k, _):
            peer = lax.rem(me_t + k, TILE)
            pltpu.make_async_remote_copy(
                src_ref=s.at[groups, :, pl.ds(24 * peer + rows.start, rows.size), :],
                dst_ref=r.at[groups, :, me_t, rows, :],
                send_sem=turn_send.at[block],
                recv_sem=turn_recv.at[block],
                device_id={"tile": peer},
                device_id_type=MESH,
            ).start()
            return 0

        lax.fori_loop(1, TILE, send, 0)

    def turn_wait(block, sems):
        groups, rows = blocks[block]
        whole = r.at[groups, :, pl.ds(0, TILE - 1), rows, :]
        pltpu.make_async_copy(whole, whole, sems.at[block]).wait()

    compress(0)
    pl.semaphore_wait(barrier, (TILE - 1) + (ACQ - 1))
    turn(0)
    compress(1)
    compress(2)
    turn(1)
    turn(2)
    own_turn = pltpu.make_async_copy(
        s.at[:, :, pl.ds(24 * me_t, 24), :], r.at[:, :, me_t], turn_own
    )
    own_turn.start()
    for copy in late:
        copy.wait()
    for n in range(4):
        wide[n] = jnp.broadcast_to(column[:, n : n + 1], (NB, 128))
    high, low = halves(left_b_f[...])
    left_b[...] = jnp.concatenate([high, high, low], axis=1)
    kept = jnp.concatenate(
        [left_b_f[FIRST : FIRST + KEPT, :], left_b_f[NB + FIRST : NB + FIRST + KEPT, :]], axis=0
    )
    high, low = halves(kept)
    left_k[...] = jnp.concatenate([high, low], axis=0)
    row = lax.broadcasted_iota(jnp.int32, (1024, 128), 0)
    col = lax.broadcasted_iota(jnp.int32, (1024, 128), 1)
    same = jnp.logical_and(col // 16 == row // 128, col % 16 == row % 128 // 8)
    value = jnp.where(same, 1.0 / 16.0, 0.0).astype(jnp.bfloat16)
    pool[...] = jnp.concatenate([value, value], axis=0)
    same = jnp.logical_and(col // 16 == row // 128, col % 16 == row % 16)
    place[...] = jnp.where(same, 1.0, 0.0).astype(jnp.bfloat16)

    def phases(j):
        for h in range(12):
            rows = pl.ds(h * 64, 64)
            a = ang[j, rows, :]
            cs[j, 0, rows, :] = jnp.cos(a) * (1.0 / NA / NR)
            cs[j, 1, rows, :] = jnp.sin(a) * (1.0 / NA / NR)

    root = float(np.sqrt(0.75))

    def butterfly(re, im, sign):
        sr, si = re[1] + re[2], im[1] + im[2]
        dr, di = (re[1] - re[2]) * (sign * root), (im[1] - im[2]) * (sign * root)
        mr, mi = re[0] - 0.5 * sr, im[0] - 0.5 * si
        return [re[0] + sr, mr - di, mr + di], [im[0] + si, mi + dr, mi - dr]

    def transform(j, groups):
        value = jnp.concatenate(
            [
                jnp.concatenate(
                    [r[a, c, :, 8 * j : 8 * j + 8, :].reshape(NB, 128) for a in groups], axis=1
                )
                for c in range(2)
            ],
            axis=0,
        )
        value = left_product(left_b[...], value)
        parts = [slice(128 * n, 128 * n + 128) for n in range(len(groups))]
        return [value[:NB, n] for n in parts], [value[NB:, n] for n in parts]

    def focus(j):
        if j < CHUNKS - 1:
            re, im = transform(j, (0, 1, 2))
        else:
            re, im = transform(j, (1, 2))
            re, im = [first_re[...]] + re, [first_im[...]] + im
        for a in (1, 2):
            tr, ti = wide[2 * a - 2], wide[2 * a - 1]
            re[a], im[a] = re[a] * tr - im[a] * ti, re[a] * ti + im[a] * tr
        re, im = butterfly(re, im, -1.0)
        for f1 in range(3):
            c, d = cs[j, 0, f1 * NB : (f1 + 1) * NB, :], cs[j, 1, f1 * NB : (f1 + 1) * NB, :]
            re[f1], im[f1] = re[f1] * c - im[f1] * d, re[f1] * d + im[f1] * c
        re, im = butterfly(re, im, 1.0)
        for a in (1, 2):
            tr, ti = wide[2 * a - 2], wide[2 * a - 1]
            re[a], im[a] = re[a] * tr + im[a] * ti, im[a] * tr - re[a] * ti
        value = jnp.concatenate([jnp.concatenate(im, axis=1), jnp.concatenate(re, axis=1)], axis=0)
        high, low = halves(value)
        value = jnp.dot(left_k[...], high, preferred_element_type=jnp.float32)
        rest = jnp.dot(left_k[: 2 * KEPT], low, preferred_element_type=jnp.float32)
        value = value[: 2 * KEPT] + (value[2 * KEPT :] + rest)
        for a in range(3):
            rows = pl.ds(8 + 3 * FIRST + a - AOI_START, 86, stride=3)
            foc[j, 1, rows, :] = value[:86, a * 128 : (a + 1) * 128]
            foc[j, 0, rows, :] = value[KEPT : KEPT + 86, a * 128 : (a + 1) * 128]

    def own_share(j):
        return pltpu.make_async_copy(
            foc.at[j, :, pl.ds(8 + me_part * PART, PART), :], gat[j].at[me_a], acq_own.at[j]
        )

    def share(j):
        def send(k, _):
            peer = lax.rem(me_a + far_first(k), ACQ)
            pltpu.make_async_remote_copy(
                src_ref=foc.at[j, :, pl.ds(8 + part_of(peer) * PART, PART), :],
                dst_ref=gat[j].at[me_a],
                send_sem=acq_send.at[j],
                recv_sem=acq_recv.at[j],
                device_id={"acq": peer},
                device_id_type=MESH,
            ).start()
            return 0

        lax.fori_loop(0, ACQ - 1, send, 0)
        own_share(j).start()

    def take_share(j):
        whole = gat[j].at[pl.ds(0, ACQ - 1)]
        pltpu.make_async_copy(whole, whole, acq_recv.at[j]).wait()
        own_share(j).wait()

    def interfere(j):
        def line_up(a, _):
            rows = pl.ds(pl.multiple_of(a * PART, PART), PART)
            for c in range(2):
                sides[2, c, rows, :] = gat[j][a, c]
                for round_id in range(2):
                    sides[round_id, c, rows, :] = gat[j][pairs[round_id, a], c]
            return 0

        lax.fori_loop(0, ACQ, line_up, 0)
        re, im = [], []
        for round_id in range(2):
            for l in range(4):
                sum_re, sum_im = 0.0, 0.0
                for o in range(2):
                    rows = pl.ds(2 * l + o, DESTS, stride=8)
                    mr, mi = sides[2, 0, rows, :], sides[2, 1, rows, :]
                    pr, pi = sides[round_id, 0, rows, :], sides[round_id, 1, rows, :]
                    sum_re += mr * pr + mi * pi
                    sum_im += mi * pr - mr * pi
                re.append(sum_re)
                im.append(sum_im)
        value = jnp.concatenate([jnp.concatenate(re, axis=1), jnp.concatenate(im, axis=1)], axis=0)
        looked = jnp.dot(
            jnp.concatenate(halves(value), axis=1), pool[...], preferred_element_type=jnp.float32
        )
        for c in range(2):
            osend[j, c] = looked[c * DESTS : (c + 1) * DESTS].reshape(DESTS, 1, 128)

    has_own = me_t // 4 == me_part

    def send_out(j, first):
        def send(d, _):
            dest_a = lax.rem(me_a + far_first(d // 4), ACQ)
            dest_t = 4 * me_part + lax.rem(d, 4)
            own = jnp.logical_and(dest_a == me_a, dest_t == me_t)

            @pl.when(jnp.logical_not(own))
            def _():
                pltpu.make_async_remote_copy(
                    src_ref=osend.at[pl.ds(first, j + 1 - first), :, 4 * dest_a + lax.rem(d, 4)],
                    dst_ref=orecv.at[pl.ds(first, j + 1 - first), :, me_t],
                    send_sem=out_send.at[j],
                    recv_sem=out_recv.at[j],
                    device_id={"acq": dest_a, "tile": dest_t},
                    device_id_type=MESH,
                ).start()

            return 0

        lax.fori_loop(0, DESTS, send, 0)

        @pl.when(has_own)
        def _():
            own_out(j, first).start()

    def own_out(j, first):
        some = pl.ds(first, j + 1 - first)
        return pltpu.make_async_copy(
            osend.at[some, :, 4 * me_a + lax.rem(me_t, 4)], orecv.at[some, :, me_t], out_own.at[j]
        )

    def out_wait(j, first, sem):
        def wait(count):
            whole = orecv.at[pl.ds(first, j + 1 - first), :, pl.ds(0, count)]
            pltpu.make_async_copy(whole, whole, sem).wait()

        @pl.when(has_own)
        def _():
            wait(DESTS - 1)

        @pl.when(jnp.logical_not(has_own))
        def _():
            wait(DESTS)

    for j in range(CHUNKS):
        phases(j)
    own_turn.wait()
    turn_wait(0, turn_recv)
    (first_re[...],), (first_im[...],) = transform(CHUNKS - 1, (0,))
    turn_wait(1, turn_recv)
    for j in range(CHUNKS):
        if j == CHUNKS - 1:
            turn_wait(2, turn_recv)
        focus(j)
        share(j)
    for j in range(CHUNKS):
        take_share(j)
        interfere(j)
        if j == 1:
            send_out(1, 0)
        if j == 2:
            send_out(2, 2)
    for j in range(CHUNKS):
        turn_wait(j, turn_send)
        whole = gat[j].at[pl.ds(0, ACQ - 1)]
        pltpu.make_async_copy(whole, whole, acq_send.at[j]).wait()
    which = lax.broadcasted_iota(jnp.int32, (8, 128), 0)
    mask = lax.broadcasted_iota(jnp.int32, (8, 128), 1) // 16 == which

    def arrange(out, chunks):
        for first_v in range(3):
            blocks = [(c, v) for c in range(2) for v in range(first_v, 12, 3)]
            ns = [n for n in range(8) if (8 * first_v + n) % CHUNKS in chunks]
            rows = []
            for c, v in blocks:
                us = [8 * v + n for n in ns]
                spread = [jnp.where(mask, orecv[u % CHUNKS, c, u // CHUNKS], 0.0) for u in us]
                rows.append(jnp.concatenate(spread, axis=1))
            table = jnp.concatenate([place[128 * n : 128 * n + 128] for n in ns], axis=0)
            high, low = halves(jnp.concatenate(rows, axis=0))
            value = jnp.dot(high, table, preferred_element_type=jnp.float32)
            value += jnp.dot(low, table, preferred_element_type=jnp.float32)
            for n, (c, v) in enumerate(blocks):
                for round_id in range(2):
                    row = (c * 2 + round_id) * 48 + 4 * v
                    first = 8 * n + 4 * round_id
                    out[row : row + 4, :] = value[first : first + 4]

    for j, first, out, chunks in ((1, 0, out_early, (0, 1)), (2, 2, out_late, (2,))):
        out_wait(j, first, out_recv.at[j])

        @pl.when(has_own)
        def _():
            own_out(j, first).wait()

        arrange(out, chunks)

    for j, first in ((1, 0), (2, 2)):
        out_wait(j, first, out_send.at[j])


def shards(unprocessed_echo_data, slant_kernel_frequencies, along_track_kernel_angle, pairs):
    echo = unprocessed_echo_data.reshape(2, GROUPS, 8, NP, NQ)
    echo = echo.transpose(0, 1, 3, 2, 4).reshape(2, GROUPS, NP * 8, NQ)
    filt = slant_kernel_frequencies.reshape(2, NP, NQ)
    angle = along_track_kernel_angle[0]
    consts = [jnp.asarray(t) for t in tables()]
    any_spec = pl.BlockSpec(memory_space=pl.ANY)
    f32 = jnp.float32
    vmem, dma = pltpu.VMEM, pltpu.SemaphoreType.DMA
    early, late = pl.pallas_call(
        kernel,
        out_shape=[vmem((2 * 2 * 12 * 4, 128), f32)] * 2,
        in_specs=[pl.BlockSpec(memory_space=pltpu.SMEM)] + [any_spec] * 8,
        out_specs=[pl.BlockSpec(memory_space=pltpu.VMEM)] * 2,
        scratch_shapes=[
            vmem((2, GROUPS, NP * 8, NQ), f32),
            vmem((GROUPS, 2, NP * 8, NQ), f32),
            vmem((GROUPS, 2, TILE, 8 * CHUNKS, 128), f32),
            vmem((CHUNKS, 2, NA, 128), f32),
            vmem((CHUNKS, NA, 128), f32),
            vmem((CHUNKS, 2, AOI + 16, 128), f32),
            vmem((ACQ, 2, PART, 128), f32),
            vmem((ACQ, 2, PART, 128), f32),
            vmem((ACQ, 2, PART, 128), f32),
            vmem((3, 2, ACQ * PART, 128), f32),
            vmem((CHUNKS, 2, DESTS, 1, 128), f32),
            vmem((CHUNKS, 2, DESTS, 1, 128), f32),
            vmem((2, NP, NQ), f32),
            vmem((NQ, 128), f32),
            vmem((2, NP, NQ), f32),
            vmem((2 * NP, 6 * NP), f32),
            vmem((2 * NQ, 2 * NQ), f32),
            vmem((2 * NB, 2 * NB), f32),
            vmem((2 * NP, 6 * NP), jnp.bfloat16),
            vmem((6 * NQ, 2 * NQ), jnp.bfloat16),
            vmem((2 * NB, 6 * NB), jnp.bfloat16),
            vmem((4 * KEPT, 2 * NB), jnp.bfloat16),
            vmem((2, NP, NQ), f32),
            vmem((NB, 128), f32),
            vmem((4, NB, 128), f32),
            vmem((2 * 8 * 128, 128), jnp.bfloat16),
            vmem((8 * 128, 128), jnp.bfloat16),
            vmem((NB, 128), f32),
            vmem((NB, 128), f32),
            dma((12,)),
            dma((CHUNKS,)),
            dma((CHUNKS,)),
            dma,
            dma((CHUNKS,)),
            dma((CHUNKS,)),
            dma((CHUNKS,)),
            dma((CHUNKS,)),
            dma((CHUNKS,)),
            dma((CHUNKS,)),
        ],
        name="range_doppler",
        compiler_params=pltpu.CompilerParams(
            collective_id=0, has_side_effects=True, vmem_limit_bytes=56 * 2**20
        ),
    )(pairs, echo, filt, angle, *consts)

    rows = (early + late).reshape(2, 2, 12, 4, 128).transpose(0, 1, 3, 2, 4)
    rows = with_layout_constraint(rows, Layout((0, 1, 3, 2, 4)))
    return rows.reshape(2, 2, 1, 4, NR // 8)


def solution(mesh):
    in_specs = (P(None, "acq", "tile", None), P(None, "acq", None), P("acq", None, "tile"), P())
    out_specs = P(None, None, "acq", "tile", None)
    return jax.shard_map(shards, mesh=mesh, in_specs=in_specs, out_specs=out_specs, check_vma=False)
```

```python
import jax
import jax.numpy as jnp
import ml_dtypes
import numpy as np
from jax import lax
from jax.experimental import pallas as pl
from jax.experimental.layout import Layout, with_layout_constraint
from jax.experimental.pallas import tpu as pltpu
from jax.sharding import PartitionSpec as P

MESH = pl.DeviceIdType.MESH
NA, NR, AOI, AOI_START = 768, 12288, 256, 256
NP, NQ = 96, 128
NB = 256
ACQ, TILE = 8, 32
GROUPS = 3
CHUNKS = 3
FIRST = AOI_START // 3
KEPT = 88
PART = AOI // ACQ
DESTS = TILE
STEPS = ((0, PART, 0), (1, PART, 0), (2, PART // 2, 0), (2, PART // 2, PART // 2))


def split3(matrix):
    high = matrix.astype(ml_dtypes.bfloat16)
    low = (matrix - high.astype(np.float64)).astype(ml_dtypes.bfloat16)
    return np.concatenate([high, high, low], axis=1).astype(np.float32)


def dft_block(size):
    ids = np.arange(size)
    angle = 2.0 * np.pi * (np.outer(ids, ids) % size) / size
    c, s = np.cos(angle), np.sin(angle)
    return np.block([[c, s], [-s, c]])


def tables():
    left_p = split3(dft_block(NP))
    right_q = dft_block(NQ).T.astype(np.float32)
    left_b = dft_block(NB).astype(np.float32)
    angle = 2.0 * np.pi * np.outer(np.arange(NP), np.arange(NQ)) / NR
    twist = np.stack([np.cos(angle), -np.sin(angle)]).astype(np.float32)
    column = np.zeros((NB, 128), np.float64)
    ids = np.arange(NB)
    for a in (1, 2):
        column[:, 2 * a - 2] = np.cos(2.0 * np.pi * a * ids / NA)
        column[:, 2 * a - 1] = -np.sin(2.0 * np.pi * a * ids / NA)
    return left_p, right_q, left_b, twist, column.astype(np.float32)


def halves(value):
    high = value.astype(jnp.bfloat16)
    return high, (value - high.astype(jnp.float32)).astype(jnp.bfloat16)


def left_product(table, value):
    high, low = halves(value)
    rhs = jnp.concatenate([high, low, high], axis=0)
    return jnp.dot(table, rhs, preferred_element_type=jnp.float32)


def right_product(value, table):
    high, low = halves(value)
    lhs = jnp.concatenate([high, low, high], axis=1)
    return jnp.dot(lhs, table, preferred_element_type=jnp.float32)


def kernel(
    pairs, echo, filt, angle, left_p_h, right_q_h, left_b_h, twist_h, column_h,
    out_early, out_late,
    x, s, r, cs, ang, foc, gat0, gat1, gat2, gat3, sides, osend, osend_last, orecv,
    fil_raw, fil_turn, fil, left_p_f, right_q_f, left_b_f, left_p, right_q, left_b, left_k, twist, column, wide, pool, place, first_re, first_im,
    in_sem, turn_send, turn_recv, turn_own, acq_send, acq_recv, acq_own, out_send, out_recv, out_own,
):
    me_a, me_t = lax.axis_index("acq"), lax.axis_index("tile")
    gat = (gat0, gat1, gat2, gat3)

    def part_of(a):
        return 2 * lax.rem(me_t // 8 + a // 2, 4) + lax.rem(a, 2)

    me_part = part_of(me_a)

    def far_first(k):
        return 4 + (k + 1) // 2 * (2 * lax.rem(k, 2) - 1)


    early = [
        pltpu.make_async_copy(left_p_h, left_p_f, in_sem.at[0]),
        pltpu.make_async_copy(right_q_h, right_q_f, in_sem.at[1]),
        pltpu.make_async_copy(filt, fil_raw, in_sem.at[2]),
        pltpu.make_async_copy(twist_h, twist, in_sem.at[3]),
    ]
    lines = [pltpu.make_async_copy(echo.at[:, i], x.at[:, i], in_sem.at[4 + i]) for i in range(3)]
    late = [
        *[
            pltpu.make_async_copy(angle.at[:, pl.ds(128 * j, 128)], ang.at[j], in_sem.at[9 + j])
            for j in range(CHUNKS)
        ],
        pltpu.make_async_copy(left_b_h, left_b_f, in_sem.at[7]),
        pltpu.make_async_copy(column_h, column, in_sem.at[8]),
    ]
    for copy in early[:2] + lines[:2] + early[2:] + lines[2:] + late:
        copy.start()

    barrier = pltpu.get_barrier_semaphore()

    def greet_tile(k, _):
        peer = lax.rem(me_t + k, TILE)
        pl.semaphore_signal(barrier, inc=1, device_id={"tile": peer}, device_id_type=MESH)
        return 0

    def greet_acq(k, _):
        peer = lax.rem(me_a + k, ACQ)
        pl.semaphore_signal(barrier, inc=1, device_id={"acq": peer}, device_id_type=MESH)
        return 0

    lax.fori_loop(1, TILE, greet_tile, 0)
    lax.fori_loop(1, ACQ, greet_acq, 0)
    early[0].wait()
    left_p[...] = left_p_f[...].astype(jnp.bfloat16)
    early[1].wait()
    high, low = halves(right_q_f[...])
    right_q[...] = jnp.concatenate([high, high, low], axis=0)
    early[2].wait()
    lane = lax.broadcasted_iota(jnp.int32, (32, 128), 1)
    for c in range(2):
        v = [fil_raw[c, pl.ds(w, 32, stride=3), :] for w in range(3)]
        fil_turn[pl.ds(0, 32, stride=4), :] = v[0]
        fil_turn[pl.ds(1, 32, stride=4), :] = jnp.where(
            lane < 32, pltpu.roll(v[0], 32, 1), pltpu.roll(v[1], 32, 1)
        )
        fil_turn[pl.ds(2, 32, stride=4), :] = jnp.where(
            lane < 64, pltpu.roll(v[1], 64, 1), pltpu.roll(v[2], 64, 1)
        )
        fil_turn[pl.ds(3, 32, stride=4), :] = pltpu.roll(v[2], 96, 1)
        fil[c] = fil_turn[...].T[:NP]
    early[3].wait()
    lines[0].wait()
    lines[1].wait()

    def compress(g):
        for part in range(2):
            if g == 0 and part == 1:
                lines[2].wait()
            ids = range(4 * part, 4 * part + 4)
            value = jnp.concatenate(
                [
                    jnp.concatenate([x[c, (3 * i + g) // 8, pl.ds((3 * i + g) % 8, NP, stride=8), :] for i in ids], axis=1)
                    for c in range(2)
                ],
                axis=0,
            )
            value = left_product(left_p[...], value)
            tr, ti = twist[0], twist[1]
            rows = []
            for n in range(4):
                re = value[:NP, n * NQ : (n + 1) * NQ]
                im = value[NP:, n * NQ : (n + 1) * NQ]
                rows.append(jnp.concatenate([re * tr - im * ti, re * ti + im * tr], axis=1))
            value = right_product(jnp.concatenate(rows, axis=0), right_q[...])
            fr, fi = fil[0], fil[1]
            rows = []
            for n in range(4):
                re = value[n * NP : (n + 1) * NP, :NQ]
                im = value[n * NP : (n + 1) * NP, NQ:]
                rows.append(jnp.concatenate([re * fi + im * fr, re * fr - im * fi], axis=1))
            value = right_product(jnp.concatenate(rows, axis=0), right_q[...])
            top, low = [], []
            for n in range(4):
                im = value[n * NP : (n + 1) * NP, :NQ]
                re = value[n * NP : (n + 1) * NP, NQ:]
                top.append(im * tr - re * ti)
                low.append(re * tr + im * ti)
            value = jnp.concatenate(
                [jnp.concatenate(top, axis=1), jnp.concatenate(low, axis=1)], axis=0
            )
            value = left_product(left_p[...], value)
            for n, i in enumerate(ids):
                s[g, 1, pl.ds(i, NP, stride=8), :] = value[:NP, n * NQ : (n + 1) * NQ]
                s[g, 0, pl.ds(i, NP, stride=8), :] = value[NP:, n * NQ : (n + 1) * NQ]

    blocks = ((pl.ds(0, 1), pl.ds(0, 24)), (pl.ds(1, 2), pl.ds(0, 16)), (pl.ds(1, 2), pl.ds(16, 8)))

    def turn(block):
        groups, rows = blocks[block]

        def send(k, _):
            peer = lax.rem(me_t + k, TILE)
            pltpu.make_async_remote_copy(
                src_ref=s.at[groups, :, pl.ds(24 * peer + rows.start, rows.size), :],
                dst_ref=r.at[groups, :, me_t, rows, :],
                send_sem=turn_send.at[block],
                recv_sem=turn_recv.at[block],
                device_id={"tile": peer},
                device_id_type=MESH,
            ).start()
            return 0

        lax.fori_loop(1, TILE, send, 0)

    def turn_wait(block, sems):
        groups, rows = blocks[block]
        whole = r.at[groups, :, pl.ds(0, TILE - 1), rows, :]
        pltpu.make_async_copy(whole, whole, sems.at[block]).wait()

    compress(0)
    pl.semaphore_wait(barrier, (TILE - 1) + (ACQ - 1))
    turn(0)
    compress(1)
    compress(2)
    turn(1)
    turn(2)
    own_turn = pltpu.make_async_copy(
        s.at[:, :, pl.ds(24 * me_t, 24), :], r.at[:, :, me_t], turn_own
    )
    own_turn.start()
    for copy in late:
        copy.wait()
    for n in range(4):
        wide[n] = jnp.broadcast_to(column[:, n : n + 1], (NB, 128))
    high, low = halves(left_b_f[...])
    left_b[...] = jnp.concatenate([high, high, low], axis=1)
    kept = jnp.concatenate(
        [left_b_f[FIRST : FIRST + KEPT, :], left_b_f[NB + FIRST : NB + FIRST + KEPT, :]], axis=0
    )
    high, low = halves(kept)
    left_k[...] = jnp.concatenate([high, low], axis=0)
    row = lax.broadcasted_iota(jnp.int32, (1024, 128), 0)
    col = lax.broadcasted_iota(jnp.int32, (1024, 128), 1)
    same = jnp.logical_and(col // 16 == row // 128, col % 16 == row % 128 // 8)
    value = jnp.where(same, 1.0 / 16.0, 0.0).astype(jnp.bfloat16)
    pool[...] = jnp.concatenate([value, value], axis=0)
    same = jnp.logical_and(col // 16 == row // 128, col % 16 == row % 16)
    place[...] = jnp.where(same, 1.0, 0.0).astype(jnp.bfloat16)

    def phases(j):
        for h in range(12):
            rows = pl.ds(h * 64, 64)
            a = ang[j, rows, :]
            cs[j, 0, rows, :] = jnp.cos(a) * (1.0 / NA / NR)
            cs[j, 1, rows, :] = jnp.sin(a) * (1.0 / NA / NR)

    root = float(np.sqrt(0.75))

    def butterfly(re, im, sign):
        sr, si = re[1] + re[2], im[1] + im[2]
        dr, di = (re[1] - re[2]) * (sign * root), (im[1] - im[2]) * (sign * root)
        mr, mi = re[0] - 0.5 * sr, im[0] - 0.5 * si
        return [re[0] + sr, mr - di, mr + di], [im[0] + si, mi + dr, mi - dr]

    def transform(j, groups):
        value = jnp.concatenate(
            [
                jnp.concatenate(
                    [r[a, c, :, 8 * j : 8 * j + 8, :].reshape(NB, 128) for a in groups], axis=1
                )
                for c in range(2)
            ],
            axis=0,
        )
        value = left_product(left_b[...], value)
        parts = [slice(128 * n, 128 * n + 128) for n in range(len(groups))]
        return [value[:NB, n] for n in parts], [value[NB:, n] for n in parts]

    def focus(j):
        if j < CHUNKS - 1:
            re, im = transform(j, (0, 1, 2))
        else:
            re, im = transform(j, (1, 2))
            re, im = [first_re[...]] + re, [first_im[...]] + im
        for a in (1, 2):
            tr, ti = wide[2 * a - 2], wide[2 * a - 1]
            re[a], im[a] = re[a] * tr - im[a] * ti, re[a] * ti + im[a] * tr
        re, im = butterfly(re, im, -1.0)
        for f1 in range(3):
            c, d = cs[j, 0, f1 * NB : (f1 + 1) * NB, :], cs[j, 1, f1 * NB : (f1 + 1) * NB, :]
            re[f1], im[f1] = re[f1] * c - im[f1] * d, re[f1] * d + im[f1] * c
        re, im = butterfly(re, im, 1.0)
        for a in (1, 2):
            tr, ti = wide[2 * a - 2], wide[2 * a - 1]
            re[a], im[a] = re[a] * tr + im[a] * ti, im[a] * tr - re[a] * ti
        value = jnp.concatenate([jnp.concatenate(im, axis=1), jnp.concatenate(re, axis=1)], axis=0)
        high, low = halves(value)
        value = jnp.dot(left_k[...], high, preferred_element_type=jnp.float32)
        rest = jnp.dot(left_k[: 2 * KEPT], low, preferred_element_type=jnp.float32)
        value = value[: 2 * KEPT] + (value[2 * KEPT :] + rest)
        for a in range(3):
            rows = pl.ds(8 + 3 * FIRST + a - AOI_START, 86, stride=3)
            foc[j, 1, rows, :] = value[:86, a * 128 : (a + 1) * 128]
            foc[j, 0, rows, :] = value[KEPT : KEPT + 86, a * 128 : (a + 1) * 128]

    def own_share(n):
        j, lines, first = STEPS[n]
        rows = pl.ds(8 + me_part * PART + first, lines)
        return pltpu.make_async_copy(foc.at[j, :, rows, :], gat[n].at[me_a], acq_own.at[n])

    def share(n):
        j, lines, first = STEPS[n]

        def send(k, _):
            peer = lax.rem(me_a + far_first(k), ACQ)
            pltpu.make_async_remote_copy(
                src_ref=foc.at[j, :, pl.ds(8 + part_of(peer) * PART + first, lines), :],
                dst_ref=gat[n].at[me_a],
                send_sem=acq_send.at[n],
                recv_sem=acq_recv.at[n],
                device_id={"acq": peer},
                device_id_type=MESH,
            ).start()
            return 0

        lax.fori_loop(0, ACQ - 1, send, 0)
        own_share(n).start()

    def take_share(n):
        whole = gat[n].at[pl.ds(0, ACQ - 1)]
        pltpu.make_async_copy(whole, whole, acq_recv.at[n]).wait()
        own_share(n).wait()

    def interfere(n):
        lines = STEPS[n][1]

        def line_up(a, _):
            rows = pl.ds(pl.multiple_of(a * lines, lines), lines)
            for c in range(2):
                sides[2, c, rows, :] = gat[n][a, c]
                for round_id in range(2):
                    sides[round_id, c, rows, :] = gat[n][pairs[round_id, a], c]
            return 0

        lax.fori_loop(0, ACQ, line_up, 0)
        re, im = [], []
        for round_id in range(2):
            for l in range(4):
                sum_re, sum_im = 0.0, 0.0
                for o in range(2):
                    rows = pl.ds(2 * l + o, lines, stride=8)
                    mr, mi = sides[2, 0, rows, :], sides[2, 1, rows, :]
                    pr, pi = sides[round_id, 0, rows, :], sides[round_id, 1, rows, :]
                    sum_re += mr * pr + mi * pi
                    sum_im += mi * pr - mr * pi
                re.append(sum_re)
                im.append(sum_im)
        value = jnp.concatenate([jnp.concatenate(re, axis=1), jnp.concatenate(im, axis=1)], axis=0)
        looked = jnp.dot(
            jnp.concatenate(halves(value), axis=1), pool[...], preferred_element_type=jnp.float32
        )
        for c in range(2):
            rows = looked[c * lines : (c + 1) * lines].reshape(lines, 1, 128)
            if n < 2:
                osend[n, c] = rows
            else:
                osend_last[n - 2, c] = rows

    has_own = me_t // 4 == me_part

    def send_looks(j, count, source, target):
        def send(d, _):
            dest_a = lax.rem(me_a + far_first(d // count), ACQ)
            i = target + lax.rem(d, count)
            dest_t = 4 * me_part + i
            own = jnp.logical_and(dest_a == me_a, dest_t == me_t)

            @pl.when(jnp.logical_not(own))
            def _():
                pltpu.make_async_remote_copy(
                    src_ref=source(count * dest_a + i - target),
                    dst_ref=looks(j),
                    send_sem=out_send.at[j],
                    recv_sem=out_recv.at[j],
                    device_id={"acq": dest_a, "tile": dest_t},
                    device_id_type=MESH,
                ).start()

            return 0

        lax.fori_loop(0, ACQ * count, send, 0)

    def looks(j):
        return orecv.at[pl.ds(0, 2) if j == 1 else pl.ds(2, 1), :, me_t]

    def send_early():
        send_looks(1, 4, lambda d: osend.at[:, :, d], 0)
        pl.when(has_own)(own_out(1).start)

    def send_last(half):
        send_looks(2, 2, lambda d: osend_last.at[pl.ds(half, 1), :, d], 2 * half)
        if half == 1:
            pl.when(has_own)(own_out(2).start)

    def own_out(j):
        i = lax.rem(me_t, 4)
        if j == 1:
            source = osend.at[:, :, 4 * me_a + i]
        else:
            source = osend_last.at[pl.ds(i // 2, 1), :, 2 * me_a + lax.rem(i, 2)]
        return pltpu.make_async_copy(source, looks(j), out_own.at[j])

    def out_wait(j, first, sem):
        def wait(count):
            whole = orecv.at[pl.ds(first, j + 1 - first), :, pl.ds(0, count)]
            pltpu.make_async_copy(whole, whole, sem).wait()

        @pl.when(has_own)
        def _():
            wait(DESTS - 1)

        @pl.when(jnp.logical_not(has_own))
        def _():
            wait(DESTS)

    for j in range(CHUNKS):
        phases(j)
    own_turn.wait()
    turn_wait(0, turn_recv)
    (first_re[...],), (first_im[...],) = transform(CHUNKS - 1, (0,))
    turn_wait(1, turn_recv)
    for j in range(CHUNKS):
        if j == CHUNKS - 1:
            turn_wait(2, turn_recv)
        focus(j)
        for n, step in enumerate(STEPS):
            if step[0] == j:
                share(n)
    for n in range(len(STEPS)):
        take_share(n)
        interfere(n)
        if n == 1:
            send_early()
        if n > 1:
            send_last(n - 2)
    for j in range(CHUNKS):
        turn_wait(j, turn_send)
    for n in range(len(STEPS)):
        whole = gat[n].at[pl.ds(0, ACQ - 1)]
        pltpu.make_async_copy(whole, whole, acq_send.at[n]).wait()
    which = lax.broadcasted_iota(jnp.int32, (8, 128), 0)
    mask = lax.broadcasted_iota(jnp.int32, (8, 128), 1) // 16 == which

    def arrange(out, chunks):
        for first_v in range(3):
            blocks = [(c, v) for c in range(2) for v in range(first_v, 12, 3)]
            ns = [n for n in range(8) if (8 * first_v + n) % CHUNKS in chunks]
            rows = []
            for c, v in blocks:
                us = [8 * v + n for n in ns]
                spread = [jnp.where(mask, orecv[u % CHUNKS, c, u // CHUNKS], 0.0) for u in us]
                rows.append(jnp.concatenate(spread, axis=1))
            table = jnp.concatenate([place[128 * n : 128 * n + 128] for n in ns], axis=0)
            high, low = halves(jnp.concatenate(rows, axis=0))
            value = jnp.dot(high, table, preferred_element_type=jnp.float32)
            value += jnp.dot(low, table, preferred_element_type=jnp.float32)
            for n, (c, v) in enumerate(blocks):
                for round_id in range(2):
                    row = (c * 2 + round_id) * 48 + 4 * v
                    first = 8 * n + 4 * round_id
                    out[row : row + 4, :] = value[first : first + 4]

    for j, first, out, chunks in ((1, 0, out_early, (0, 1)), (2, 2, out_late, (2,))):
        out_wait(j, first, out_recv.at[j])

        @pl.when(has_own)
        def _():
            own_out(j).wait()

        arrange(out, chunks)

    for j, first in ((1, 0), (2, 2)):
        out_wait(j, first, out_send.at[j])


def shards(unprocessed_echo_data, slant_kernel_frequencies, along_track_kernel_angle, pairs):
    echo = unprocessed_echo_data.reshape(2, GROUPS, 8, NP, NQ)
    echo = echo.transpose(0, 1, 3, 2, 4).reshape(2, GROUPS, NP * 8, NQ)
    filt = slant_kernel_frequencies.reshape(2, NP, NQ)
    angle = along_track_kernel_angle[0]
    consts = [jnp.asarray(t) for t in tables()]
    any_spec = pl.BlockSpec(memory_space=pl.ANY)
    f32 = jnp.float32
    vmem, dma = pltpu.VMEM, pltpu.SemaphoreType.DMA
    early, late = pl.pallas_call(
        kernel,
        out_shape=[vmem((2 * 2 * 12 * 4, 128), f32)] * 2,
        in_specs=[pl.BlockSpec(memory_space=pltpu.SMEM)] + [any_spec] * 8,
        out_specs=[pl.BlockSpec(memory_space=pltpu.VMEM)] * 2,
        scratch_shapes=[
            vmem((2, GROUPS, NP * 8, NQ), f32),
            vmem((GROUPS, 2, NP * 8, NQ), f32),
            vmem((GROUPS, 2, TILE, 8 * CHUNKS, 128), f32),
            vmem((CHUNKS, 2, NA, 128), f32),
            vmem((CHUNKS, NA, 128), f32),
            vmem((CHUNKS, 2, AOI + 16, 128), f32),
            *[vmem((ACQ, 2, step[1], 128), f32) for step in STEPS],
            vmem((3, 2, ACQ * PART, 128), f32),
            vmem((2, 2, DESTS, 1, 128), f32),
            vmem((2, 2, DESTS // 2, 1, 128), f32),
            vmem((CHUNKS, 2, DESTS, 1, 128), f32),
            vmem((2, NP, NQ), f32),
            vmem((NQ, 128), f32),
            vmem((2, NP, NQ), f32),
            vmem((2 * NP, 6 * NP), f32),
            vmem((2 * NQ, 2 * NQ), f32),
            vmem((2 * NB, 2 * NB), f32),
            vmem((2 * NP, 6 * NP), jnp.bfloat16),
            vmem((6 * NQ, 2 * NQ), jnp.bfloat16),
            vmem((2 * NB, 6 * NB), jnp.bfloat16),
            vmem((4 * KEPT, 2 * NB), jnp.bfloat16),
            vmem((2, NP, NQ), f32),
            vmem((NB, 128), f32),
            vmem((4, NB, 128), f32),
            vmem((2 * 8 * 128, 128), jnp.bfloat16),
            vmem((8 * 128, 128), jnp.bfloat16),
            vmem((NB, 128), f32),
            vmem((NB, 128), f32),
            dma((12,)),
            dma((CHUNKS,)),
            dma((CHUNKS,)),
            dma,
            dma((len(STEPS),)),
            dma((len(STEPS),)),
            dma((len(STEPS),)),
            dma((CHUNKS,)),
            dma((CHUNKS,)),
            dma((CHUNKS,)),
        ],
        name="range_doppler",
        compiler_params=pltpu.CompilerParams(
            collective_id=0, has_side_effects=True, vmem_limit_bytes=56 * 2**20
        ),
    )(pairs, echo, filt, angle, *consts)

    rows = (early + late).reshape(2, 2, 12, 4, 128).transpose(0, 1, 3, 2, 4)
    rows = with_layout_constraint(rows, Layout((0, 1, 3, 2, 4)))
    return rows.reshape(2, 2, 1, 4, NR // 8)


def solution(mesh):
    in_specs = (P(None, "acq", "tile", None), P(None, "acq", None), P("acq", None, "tile"), P())
    out_specs = P(None, None, "acq", "tile", None)
    return jax.shard_map(shards, mesh=mesh, in_specs=in_specs, out_specs=out_specs, check_vma=False)
```
